32 devices in a mesh: pipe: 2 (over x), dp: 4 (over z), row: 2 (over core), col: 2 (over y).
Axes of the slice: x: 2, y: 2, z: 4, core: 2. Of those that a mesh axis runs over, the one named last changes fastest.
Arguments:
- images: bfloat16 [16, 196, 512], P(('dp', 'row'), 'col'), may hold values from -6 to 6
- extents: int32 [16, 2], P(('dp', 'row')), may hold values from 8 to 14
- cotangent: bfloat16 [16, 196, 512], P(('dp', 'row'), 'col'), may hold values from -6 to 6
- qkv_weight: bfloat16 [2, 512, 3, 512], P('pipe', 'row', None, 'col'), may hold values from -0.25 to 0.25
- qkv_bias: float32 [2, 2, 512], P('pipe', None, 'col'), may hold values from -3 to 3
- proj_weight: bfloat16 [2, 512, 512], P('pipe', 'col', 'row'), may hold values from -1 to 1
- proj_bias: float32 [2, 512], P('pipe'), may hold values from -3 to 3
- fc1_weight: bfloat16 [2, 512, 2048], P('pipe', 'row', 'col'), may hold values from -0.25 to 0.25
- fc1_bias: float32 [2, 2048], P('pipe', 'col'), may hold values from -3 to 3
- fc2_weight: bfloat16 [2, 2048, 512], P('pipe', 'col', 'row'), may hold values from -0.125 to 0.125
- fc2_bias: float32 [2, 512], P('pipe'), may hold values from -3 to 3
- norm_gain: float32 [2, 2, 512], P('pipe'), may hold values from 0.5 to 1.5
- norm_bias: float32 [2, 2, 512], P('pipe'), may hold values from -3 to 3
- bias_table: float32 [2, 169, 16], P('pipe', None, 'col'), may hold values from -5 to 5
Outputs:
- layer_outputs: bfloat16 [2, 16, 196, 512], P('pipe', ('dp', 'row'), 'col')
- input_grads: bfloat16 [2, 16, 196, 512], P('pipe', ('dp', 'row'), 'col')
- qkv_weight_grad: float32 [2, 512, 3, 512], P('pipe', 'row', None, 'col')
- qkv_bias_grad: float32 [2, 2, 512], P('pipe', None, 'col')
- proj_weight_grad: float32 [2, 512, 512], P('pipe', 'col', 'row')
- proj_bias_grad: float32 [2, 512], P('pipe')
- fc1_weight_grad: float32 [2, 512, 2048], P('pipe', 'row', 'col')
- fc1_bias_grad: float32 [2, 2048], P('pipe', 'col')
- fc2_weight_grad: float32 [2, 2048, 512], P('pipe', 'col', 'row')
- fc2_bias_grad: float32 [2, 512], P('pipe')
- norm_gain_grad: float32 [2, 2, 512], P('pipe')
- norm_bias_grad: float32 [2, 2, 512], P('pipe')
- table_grad: float32 [2, 169, 16], P('pipe', None, 'col')
The draws below stay inside these ranges and needn't reach their ends.
All inputs are finite; a program needn't handle non-finite values.
Results may differ from the reference program's by a relative error of at most 0.022.
Values may be sent and summed in bfloat16 or wider, within the bound.
A program may use at most 128 MiB of HBM per device.

```python
import jax
import jax.numpy as jnp
from jax import lax

D = 512
HEADS = 16
FF = 2048
HEAD_DIM = 32
WINDOW = 7
SIDE = 14
SHIFT = 3
SPAN = 13
TABLE = 169
PATCHES = 196
IMAGES = 16


def set_ends(values, own_key, smallest, top_value):
    extent = values.shape
    spot = [jax.random.randint(jax.random.fold_in(own_key, axis), (), 0, extent[axis]) for axis in range(len(extent))]
    values = values.at[tuple(spot)].set(smallest)
    longest = extent.index(max(extent))
    spot[longest] = (spot[longest] + 1) % extent[longest]
    return values.at[tuple(spot)].set(top_value)


def block_levels(rng, shape, shards, smallest, largest):
    loudness = 1.0
    for dim, blocks in shards:
        heights = jax.random.uniform(jax.random.fold_in(jax.random.fold_in(rng, 6), dim), (blocks,), jnp.float32, smallest / len(shards), largest / len(shards))
        loudness = loudness * jnp.repeat(jnp.exp(heights), shape[dim] // blocks).reshape((-1,) + (1,) * (len(shape) - 1 - dim))
    return loudness


def gaussian(key, dims, spread, bound, split=(), held_as=jnp.bfloat16):
    array = spread * jax.random.normal(key, dims, jnp.float32)
    if split:
        array = array * block_levels(key, dims, split, -0.22, 0.18)
    return jnp.clip(array, -bound, bound).astype(held_as)


def setup_inputs(seed: int = 0) -> dict:
    seeds = jax.random.split(jax.random.key(seed), 15)
    return {
        "images": gaussian(seeds[0], (IMAGES, PATCHES, D), 1.0, 6.0, ((0, 8), (1, 2))),
        "extents": set_ends(jax.random.randint(seeds[1], (IMAGES, 2), 8, 15), jax.random.fold_in(seeds[1], 1), 8, 14).astype(jnp.int32),
        "cotangent": gaussian(seeds[2], (IMAGES, PATCHES, D), 1.0, 6.0, ((0, 8), (1, 2))),
        "qkv_weight": gaussian(seeds[3], (2, D, 3, D), D ** -0.5, 0.25, ((0, 2), (1, 2), (3, 2))),
        "qkv_bias": gaussian(seeds[4], (2, 2, D), 0.5, 3.0, ((0, 2), (2, 2)), jnp.float32),
        "proj_weight": gaussian(seeds[5], (2, D, D), (D // 16) ** -0.5, 1.0, ((0, 2), (1, 2), (2, 2))),
        "proj_bias": gaussian(seeds[6], (2, D), 0.5, 3.0, ((0, 2),), jnp.float32),
        "fc1_weight": gaussian(seeds[7], (2, D, FF), D ** -0.5, 0.25, ((0, 2), (1, 2), (2, 2))),
        "fc1_bias": gaussian(seeds[8], (2, FF), 0.5, 3.0, ((0, 2), (1, 2)), jnp.float32),
        "fc2_weight": gaussian(seeds[9], (2, FF, D), FF ** -0.5, 0.125, ((0, 2), (1, 2), (2, 2))),
        "fc2_bias": gaussian(seeds[10], (2, D), 0.5, 3.0, ((0, 2),), jnp.float32),
        "norm_gain": jnp.clip(1.0 + 0.1 * jax.random.normal(seeds[11], (2, 2, D), jnp.float32), 0.5, 1.5),
        "norm_bias": gaussian(seeds[12], (2, 2, D), 0.5, 3.0, ((0, 2),), jnp.float32),
        "bias_table": gaussian(seeds[13], (2, TABLE, HEADS), 1.0, 5.0, ((0, 2), (2, 2)), jnp.float32),
    }


exact_precision = lax.Precision.HIGHEST
blocked_value = -1000000000.0
images_per_block = 16

@jax.custom_vjp
def low(v):
    return lax.optimization_barrier(v.astype(jnp.bfloat16)).astype(jnp.float32)

@jax.custom_vjp
def low_back(v):
    return v

def low_keep(v):
    return (low(v), None)

def low_pass(kept, grad):
    return (grad,)

def back_keep(v):
    return (v, None)

def back_low(kept, grad):
    return (low(grad),)
low.defvjp(low_keep, low_pass)
low_back.defvjp(back_keep, back_low)

def layer_norm(values, gain, offset):
    row_mean = lax.optimization_barrier(jnp.mean(values, -1, keepdims=True))
    centred = values - row_mean
    variance = lax.optimization_barrier(jnp.mean(centred * centred, -1, keepdims=True))
    return centred * lax.rsqrt(variance + 1e-05) * gain + offset

def to_windows(token_rows, offset_cells):
    image_count = token_rows.shape[0]
    features = token_rows.shape[-1]
    cell_grid = token_rows.reshape(image_count, SIDE, SIDE, features)
    cell_grid = jnp.roll(cell_grid, -offset_cells, axis=1)
    cell_grid = jnp.roll(cell_grid, -offset_cells, axis=2)
    cell_grid = cell_grid.reshape(image_count, SIDE // WINDOW, WINDOW, SIDE // WINDOW, WINDOW, features)
    cell_grid = cell_grid.transpose(0, 1, 3, 2, 4, 5)
    return cell_grid.reshape(image_count * (SIDE // WINDOW) ** 2, WINDOW * WINDOW, features)

def from_windows(window_rows, offset_cells, image_count):
    features = window_rows.shape[-1]
    cell_grid = window_rows.reshape(image_count, SIDE // WINDOW, SIDE // WINDOW, WINDOW, WINDOW, features)
    cell_grid = cell_grid.transpose(0, 1, 3, 2, 4, 5).reshape(image_count, SIDE, SIDE, features)
    cell_grid = jnp.roll(cell_grid, offset_cells, axis=1)
    cell_grid = jnp.roll(cell_grid, offset_cells, axis=2)
    return cell_grid.reshape(image_count, SIDE * SIDE, features)

def window_codes(extents, shift_flag):
    places = jnp.arange(SIDE, dtype=jnp.int32)
    source = (places + SHIFT * shift_flag) % SIDE
    padded = (source[None, :, None] >= extents[:, 0, None, None]) | (source[None, None, :] >= extents[:, 1, None, None])
    band_index = (places >= SIDE - WINDOW).astype(jnp.int32) + (places >= SIDE - SHIFT).astype(jnp.int32)
    region_codes = (band_index[:, None] * 3 + band_index[None, :]) * shift_flag * 2 + padded.astype(jnp.int32)
    image_count = extents.shape[0]
    region_codes = region_codes.reshape(image_count, SIDE // WINDOW, WINDOW, SIDE // WINDOW, WINDOW).transpose(0, 1, 3, 2, 4)
    return region_codes.reshape(image_count * (SIDE // WINDOW) ** 2, WINDOW * WINDOW)

def relative_index():
    window_cells = jnp.arange(WINDOW * WINDOW, dtype=jnp.int32)
    cell_rows = window_cells // WINDOW
    cell_cols = window_cells % WINDOW
    return (cell_rows[:, None] - cell_rows[None, :] + WINDOW - 1) * SPAN + cell_cols[:, None] - cell_cols[None, :] + WINDOW - 1

def swin_layer(hidden_in, extents, params, shift_flag):
    norm_gains, offsets, qkv_w, qkv_b, proj_w, proj_b, fc1_w, fc1_b, fc2_w, fc2_b, table = params
    image_count = hidden_in.shape[0]
    offset_cells = SHIFT * shift_flag
    normed = low(layer_norm(hidden_in, norm_gains[0], offsets[0]))
    windows = to_windows(normed, offset_cells)
    win_count = windows.shape[0]
    qkv_terms = jnp.einsum('wtd,dce->wtce', windows, qkv_w, precision=exact_precision)
    qkv_terms = qkv_terms + jnp.stack([qkv_b[0], jnp.zeros_like(qkv_b[0]), qkv_b[1]], 0)
    qkv_terms = low(low_back(qkv_terms))
    head_split = qkv_terms.reshape(win_count, WINDOW * WINDOW, 3, HEADS, HEAD_DIM)
    query_heads = head_split[:, :, 0]
    key_heads = head_split[:, :, 1]
    value_heads = head_split[:, :, 2]
    rel_bias = table[relative_index()].transpose(0, 2, 1)
    scores = HEAD_DIM ** (-0.5) * jnp.einsum('wqhd,wkhd->wqhk', query_heads, key_heads, precision=exact_precision) + rel_bias
    scores = low_back(scores)
    region_codes = window_codes(extents, shift_flag)
    allowed = region_codes[:, :, None] == region_codes[:, None, :]
    scores = jnp.where(allowed[:, :, None, :], scores, blocked_value)
    attn_probs = jax.nn.softmax(scores, axis=-1)
    mixed_heads = jnp.einsum('wqhk,wkhd->wqhd', low(attn_probs), value_heads, precision=exact_precision)
    mixed_heads = low(low_back(mixed_heads.reshape(win_count, WINDOW * WINDOW, D)))
    attention = jnp.einsum('wte,ef->wtf', mixed_heads, proj_w, precision=exact_precision) + proj_b
    attention = low_back(attention)
    middle = hidden_in + from_windows(attention, offset_cells, image_count)
    normed_two = low(layer_norm(middle, norm_gains[1], offsets[1]))
    pre_act = jnp.einsum('ntd,df->ntf', normed_two, fc1_w, precision=exact_precision) + fc1_b
    pre_act = low_back(pre_act)
    activation = low(jax.nn.gelu(pre_act, approximate=False))
    branch = jnp.einsum('ntf,fd->ntd', activation, fc2_w, precision=exact_precision) + fc2_b
    branch = low_back(branch)
    return middle + branch

def reference(images, extents, cotangent, qkv_weight, qkv_bias, proj_weight, proj_bias, fc1_weight, fc1_bias, fc2_weight, fc2_bias, norm_gain, norm_bias, bias_table):
    stacked = tuple((array_item.astype(jnp.float32) for array_item in (norm_gain, norm_bias, qkv_weight, qkv_bias, proj_weight, proj_bias, fc1_weight, fc1_bias, fc2_weight, fc2_bias, bias_table)))
    params_one = tuple((array_item[0] for array_item in stacked))
    params_two = tuple((array_item[1] for array_item in stacked))
    block_count = IMAGES // images_per_block
    blocked = (images.reshape(block_count, images_per_block, PATCHES, D), extents.reshape(block_count, images_per_block, 2), cotangent.reshape(block_count, images_per_block, PATCHES, D))
    zero_one = jax.tree.map(jnp.zeros_like, params_one)
    zero_two = jax.tree.map(jnp.zeros_like, params_two)

    def step_block(grad_carry, image_block):
        block_images, block_extents, block_cot = image_block

        def layer_zero(hidden_in, params):
            return swin_layer(hidden_in, block_extents, params, 0)

        def layer_first(hidden_in, params):
            return swin_layer(hidden_in, block_extents, params, 1)
        out_one, back_one = jax.vjp(layer_zero, block_images.astype(jnp.float32), params_one)
        passed = low(out_one)
        out_two, back_two = jax.vjp(layer_first, passed, params_two)
        grad_mid, grads_two = back_two(block_cot.astype(jnp.float32))
        grad_mid = low(grad_mid)
        grad_in, grads_one = back_one(grad_mid)
        new_carry = (jax.tree.map(jnp.add, grad_carry[0], grads_one), jax.tree.map(jnp.add, grad_carry[1], grads_two))
        return (new_carry, (out_one.astype(jnp.bfloat16), out_two.astype(jnp.bfloat16), grad_in.astype(jnp.bfloat16), grad_mid.astype(jnp.bfloat16)))
    grad_totals, results = lax.scan(step_block, (zero_one, zero_two), blocked)
    out_one, out_two, grad_in, grad_mid = results
    layer_outputs = jnp.stack([out_one.reshape(IMAGES, PATCHES, D), out_two.reshape(IMAGES, PATCHES, D)], 0)
    input_grads = jnp.stack([grad_in.reshape(IMAGES, PATCHES, D), grad_mid.reshape(IMAGES, PATCHES, D)], 0)
    joined = tuple((jnp.stack([grad_one, grad_two], 0) for grad_one, grad_two in zip(grad_totals[0], grad_totals[1])))
    gain_grad, offset_grad, qkv_grad, qkv_bias_grad, proj_grad, proj_bias_grad, fc1_grad, fc1_bias_grad, fc2_grad, fc2_bias_grad, table_grad = joined
    return (layer_outputs, input_grads, qkv_grad, qkv_bias_grad, proj_grad, proj_bias_grad, fc1_grad, fc1_bias_grad, fc2_grad, fc2_bias_grad, gain_grad, offset_grad, table_grad)
```

```python
import jax
import jax.numpy as jnp
import numpy as np
from jax import lax
from jax.experimental import pallas as pl
from jax.experimental.pallas import tpu as pltpu
from jax.sharding import PartitionSpec as P

D = 512
HEADS = 16
FF = 2048
HEAD_DIM = 32
WINDOW = 7
CELLS = 49
SIDE = 14
SHIFT = 3
SPAN = 13
TABLE = 169
PAD = 64
HALF_ROWS = 7
KEPT = 56
B = 256
SCALE = HEAD_DIM ** (-0.5)
EPS = 1e-05
BLOCKED = -1000000000.0
BF = jnp.bfloat16
F32 = jnp.float32


def nn(a, b):
    return lax.dot_general(a, b, (((1,), (0,)), ((), ())), preferred_element_type=F32)


def nt(a, b):
    return lax.dot_general(a, b, (((1,), (1,)), ((), ())), preferred_element_type=F32)


def tn(a, b):
    return lax.dot_general(a, b, (((0,), (0,)), ((), ())), preferred_element_type=F32)


def norm_parts(values):
    mean = jnp.mean(values, -1, keepdims=True)
    centred = values - mean
    inv = lax.rsqrt(jnp.mean(centred * centred, -1, keepdims=True) + EPS)
    return centred * inv, inv


def norm_back(grad, values, gain):
    x, inv = norm_parts(values)
    s = grad * gain
    back = (s - jnp.mean(s, -1, keepdims=True) - x * jnp.mean(s * x, -1, keepdims=True)) * inv
    return back, x


def head_mask(dtype):
    lane = lax.broadcasted_iota(jnp.int32, (4 * PAD, 128), 1) // HEAD_DIM
    row = lax.broadcasted_iota(jnp.int32, (4 * PAD, 128), 0) // PAD
    return (lane == row).astype(F32).astype(dtype)


def four(x):
    return jnp.concatenate([x, x, x, x], axis=0)


def fold(x, mask):
    y = x * mask
    return y[:PAD] + y[PAD : 2 * PAD] + y[2 * PAD : 3 * PAD] + y[3 * PAD :]


def cut(j):
    return slice(j * B, (j + 1) * B)


def attn_fwd(win, h, allow, rel, w, qb, pb, gains, offs, normed, qkv, probs, mixed, middle):
    hv = h[...].astype(F32)
    x, _ = norm_parts(hv)
    nv = (x * gains[0:1] + offs[0:1]).astype(BF)
    normed[...] = nv
    for c in range(2):
        for t in range(3):
            acc = nn(nv[:, cut(0)], w[0, c, t]) + nn(nv[:, cut(1)], w[1, c, t])
            qkv[c, :, cut(t)] = (acc + qb[c : c + 1, cut(t)]).astype(BF)
    mask_low = head_mask(BF)
    mask = head_mask(F32)
    for c in range(2):
        for g in range(2):
            grp = 2 * c + g
            for n in range(win):
                rows = slice(n * PAD, (n + 1) * PAD)
                q = qkv[c, rows, g * 128 : g * 128 + 128]
                k = qkv[c, rows, B + g * 128 : B + g * 128 + 128]
                v = qkv[c, rows, 2 * B + g * 128 : 2 * B + g * 128 + 128]
                s = nt(four(q) * mask_low, k) * SCALE + rel[grp]
                s = jnp.where(allow[n] > 0.5, s, BLOCKED)
                e = jnp.exp(s - jnp.max(s, -1, keepdims=True))
                p = e / jnp.sum(e, -1, keepdims=True)
                probs[n * 4 + grp] = p
                o = fold(nn(p.astype(BF), v), mask)
                mixed[rows, grp * 128 : grp * 128 + 128] = o.astype(BF)
    mv = mixed[...]
    for r in range(2):
        acc = nn(mv[:, cut(0)], w[r, 0, 3]) + nn(mv[:, cut(1)], w[r, 1, 3])
        middle[:, cut(r)] = hv[:, cut(r)] + (acc + pb[:, cut(r)])


def mlp_fwd(middle, w, b1, b2, gains, offs, n2, act, dact, out):
    mv = middle[...]
    x, _ = norm_parts(mv)
    nv = (x * gains[1:2] + offs[1:2]).astype(BF)
    n2[...] = nv
    acc = [mv[:, cut(r)] + b2[:, cut(r)] for r in range(2)]
    for c in range(2):
        for j in range(4):
            cols = slice(c * 1024 + j * B, c * 1024 + (j + 1) * B)
            pre = nn(nv[:, cut(0)], w[0, c, j]) + nn(nv[:, cut(1)], w[1, c, j]) + b1[:, cols]
            phi = 0.5 + 0.5 * lax.erf(pre * (0.5 ** 0.5))
            av = (pre * phi).astype(BF)
            act[:, cols] = av
            dact[:, cols] = phi + pre * (jnp.exp(-0.5 * pre * pre) * 0.3989422804014327)
            for r in range(2):
                acc[r] = acc[r] + nn(av, w[r, c, 4 + j])
    for r in range(2):
        out[:, cut(r)] = acc[r].astype(BF)


def mlp_bwd(full, g_out, act, dact, n2, middle, w, gains, *outs):
    gz = g_out[...]
    gn = [None, None]
    for c in range(2):
        for j in range(4):
            cols = slice(c * 1024 + j * B, c * 1024 + (j + 1) * B)
            ga = nt(gz[:, cut(0)], w[0, c, 4 + j]) + nt(gz[:, cut(1)], w[1, c, 4 + j])
            gp = (ga * dact[:, cols]).astype(BF)
            for r in range(2):
                t = nt(gp, w[r, c, j])
                gn[r] = t if gn[r] is None else gn[r] + t
            if full:
                av = act[:, cols]
                outs[2][:, cols] = jnp.sum(gp.astype(F32), 0, keepdims=True)
                for r in range(2):
                    outs[1][r, c, 4 + j] = tn(av, gz[:, cut(r)]).astype(BF)
                    outs[1][r, c, j] = tn(n2[:, cut(r)], gp).astype(BF)
    gnv = jnp.concatenate(gn, axis=1)
    back, x = norm_back(gnv, middle[...], gains[1:2])
    gf = gz.astype(F32)
    outs[0][...] = gf + back
    if full:
        outs[3][0:1] = jnp.sum(gnv * x, 0, keepdims=True)
        outs[3][1:2] = jnp.sum(gnv, 0, keepdims=True)
        outs[3][2:3] = jnp.sum(gf, 0, keepdims=True)


def attn_bwd(full, win, gm, mixed, qkv, probs, normed, h, w, gains, *rest):
    outs, (gmix, gqkv) = rest[:-2], rest[-2:]
    gmv = gm[...]
    ga = gmv.astype(BF)
    for c in range(2):
        acc = nt(ga[:, cut(0)], w[0, c, 3]) + nt(ga[:, cut(1)], w[1, c, 3])
        gmix[:, cut(c)] = acc.astype(BF)
    mask_low = head_mask(BF)
    mask = head_mask(F32)
    for c in range(2):
        for g in range(2):
            grp = 2 * c + g
            total = None
            for n in range(win):
                rows = slice(n * PAD, (n + 1) * PAD)
                q = qkv[c, rows, g * 128 : g * 128 + 128]
                k = qkv[c, rows, B + g * 128 : B + g * 128 + 128]
                v = qkv[c, rows, 2 * B + g * 128 : 2 * B + g * 128 + 128]
                g4 = four(gmix[rows, grp * 128 : grp * 128 + 128]) * mask_low
                p = probs[n * 4 + grp]
                gp = nt(g4, v)
                ds = (p * (gp - jnp.sum(p * gp, -1, keepdims=True))).astype(BF)
                gv = tn(p.astype(BF), g4)
                gq = fold(nn(ds, k), mask) * SCALE
                gk = tn(ds, four(q) * mask_low) * SCALE
                gqkv[c, rows, g * 128 : g * 128 + 128] = gq.astype(BF)
                gqkv[c, rows, B + g * 128 : B + g * 128 + 128] = gk.astype(BF)
                gqkv[c, rows, 2 * B + g * 128 : 2 * B + g * 128 + 128] = gv.astype(BF)
                if full:
                    total = ds.astype(F32) if total is None else total + ds.astype(F32)
            if full:
                outs[4][grp] = total
    gn = [None, None]
    for c in range(2):
        for t in range(3):
            gt = gqkv[c, :, cut(t)]
            for r in range(2):
                part = nt(gt, w[r, c, t])
                gn[r] = part if gn[r] is None else gn[r] + part
                if full:
                    outs[1][r, c, t] = tn(normed[:, cut(r)], gt).astype(BF)
            if full:
                outs[2][c : c + 1, cut(t)] = jnp.sum(gt.astype(F32), 0, keepdims=True)
    gnv = jnp.concatenate(gn, axis=1)
    back, x = norm_back(gnv, h[...].astype(F32), gains[0:1])
    outs[0][...] = (gmv + back).astype(BF)
    if full:
        for c in range(2):
            for r in range(2):
                outs[1][r, c, 3] = tn(mixed[:, cut(c)], ga[:, cut(r)]).astype(BF)
        outs[3][0:1] = jnp.sum(gnv * x, 0, keepdims=True)
        outs[3][1:2] = jnp.sum(gnv, 0, keepdims=True)
        outs[3][2:3] = jnp.sum(ga.astype(F32), 0, keepdims=True)


def run(body, args, outs, name, flops, scratch=()):
    shapes = [jax.ShapeDtypeStruct(s, d) for s, d in outs]
    moved = sum(a.size * a.dtype.itemsize for a in list(args) + shapes)
    vm = pl.BlockSpec(memory_space=pltpu.VMEM)
    return pl.pallas_call(
        body,
        out_shape=shapes,
        in_specs=[vm] * len(args),
        out_specs=[vm] * len(outs),
        scratch_shapes=list(scratch),
        compiler_params=pltpu.CompilerParams(vmem_limit_bytes=48 * 1024 * 1024),
        cost_estimate=pl.CostEstimate(flops=flops, bytes_accessed=moved, transcendentals=0),
        name=name,
    )(*args)


def place_matrix(images, shift):
    out = np.zeros((images * 2 * PAD, images * 98), np.float32)
    for n in range(images):
        for r in range(HALF_ROWS):
            for c in range(SIDE):
                rolled = (c - shift) % SIDE
                row = (n * 2 + rolled // WINDOW) * PAD + r * WINDOW + rolled % WINDOW
                out[row, n * 98 + r * SIDE + c] = 1.0
    return out


def allowed_cells(extents, section, col):
    images = extents.shape[0]
    places = jnp.arange(SIDE, dtype=jnp.int32)
    source = (places + SHIFT * section) % SIDE
    padded = (source[None, :, None] >= extents[:, 0, None, None]) | (
        source[None, None, :] >= extents[:, 1, None, None]
    )
    band = (places >= SIDE - WINDOW).astype(jnp.int32) + (places >= SIDE - SHIFT).astype(jnp.int32)
    codes = (band[:, None] * 3 + band[None, :]) * section * 2 + padded.astype(jnp.int32)
    mine = lax.dynamic_slice_in_dim(codes, col * HALF_ROWS, HALF_ROWS, 1)
    mine = mine.reshape(images, HALF_ROWS, 2, WINDOW).transpose(0, 2, 1, 3)
    mine = mine.reshape(images * 2, CELLS)
    query = jnp.pad(mine, ((0, 0), (0, PAD - CELLS)))
    key = jnp.pad(mine, ((0, 0), (0, PAD - CELLS)), constant_values=-1)
    real = jnp.arange(PAD) < CELLS
    same = (query[:, :, None] == key[:, None, :]) | ((~real)[None, :, None] & real[None, None, :])
    return jnp.tile(same.astype(F32), (1, 4, 1))


def relative_onehot():
    cells = np.arange(CELLS)
    a, b = cells // WINDOW, cells % WINDOW
    index = (a[:, None] - a[None, :] + WINDOW - 1) * SPAN + b[:, None] - b[None, :] + WINDOW - 1
    full = np.full((PAD, PAD), -1, np.int32)
    full[:CELLS, :CELLS] = index
    return jnp.asarray(full.reshape(-1))[None, :] == jnp.arange(TABLE, dtype=jnp.int32)[:, None]


def per_device(
    images,
    extents,
    cotangent,
    qkv_weight,
    qkv_bias,
    proj_weight,
    proj_bias,
    fc1_weight,
    fc1_bias,
    fc2_weight,
    fc2_bias,
    norm_gain,
    norm_bias,
    bias_table,
):
    section = lax.axis_index("pipe")
    row = lax.axis_index("row")
    col = lax.axis_index("col")
    first = section == 0
    count = images.shape[0]
    win = count * 2
    rows = win * PAD

    def swap(x, axis):
        return lax.ppermute(x, axis, [(0, 1), (1, 0)])

    attn_w = jnp.concatenate(
        [qkv_weight[0].transpose(1, 0, 2), proj_weight], axis=0
    )
    mlp_w = jnp.concatenate(
        [fc1_weight[0].reshape(B, 4, B).transpose(1, 0, 2), fc2_weight[0].reshape(4, B, B)], axis=0
    )

    def gather_weights(x):
        x = lax.all_gather(x, "col", axis=0)
        return lax.all_gather(x, "row", axis=0)

    attn_w = gather_weights(attn_w)
    mlp_w = gather_weights(mlp_w)
    zeros = jnp.zeros_like(qkv_bias[0, 0])
    packed = jnp.concatenate(
        [qkv_bias[0, 0], zeros, qkv_bias[0, 1], fc1_bias[0], bias_table[0].T.reshape(-1)]
    )
    packed = lax.all_gather(packed, "col", axis=0)
    qb = packed[:, :768]
    b1 = packed[:, 768:1792].reshape(1, FF)
    table = packed[:, 1792:].reshape(HEADS, TABLE)
    pb, b2, gains, offs = proj_bias, fc2_bias, norm_gain[0], norm_bias[0]
    onehot = relative_onehot().astype(F32)
    rel = jnp.dot(table, onehot, precision=lax.Precision.HIGHEST).reshape(4, 4 * PAD, PAD)
    allow = allowed_cells(extents, section, col)
    place = jnp.where(
        first, jnp.asarray(place_matrix(count, 0), BF), jnp.asarray(place_matrix(count, SHIFT), BF)
    )

    def to_win(nat):
        return nn(place, nat.reshape(count * 98, D)).astype(BF)

    def from_win(x):
        return tn(place, x).astype(BF).reshape(count, 98, D)

    def forward(h):
        normed, qkv, probs, mixed, middle = run(
            lambda *a: attn_fwd(win, *a),
            (h, allow, rel, attn_w, qb, pb, gains, offs),
            [
                ((rows, D), BF),
                ((2, rows, 768), BF),
                ((win * 4, 4 * PAD, PAD), F32),
                ((rows, D), BF),
                ((rows, D), F32),
            ],
            "attn_fwd",
            2 * rows * D * D * 4,
        )
        n2, act, dact, out = run(
            mlp_fwd,
            (middle, mlp_w, b1, b2, gains, offs),
            [((rows, D), BF), ((rows, FF), BF), ((rows, FF), F32), ((rows, D), BF)],
            "mlp_fwd",
            2 * rows * D * FF * 2,
        )
        return (h, normed, qkv, probs, mixed, middle, n2, act, dact), from_win(out)

    def backward(kept, g_out, full):
        h, normed, qkv, probs, mixed, middle, n2, act, dact = kept
        extra = [((2, 2, 8, B, B), BF), ((1, FF), F32), ((3, D), F32)] if full else []
        res = run(
            lambda *a: mlp_bwd(full, *a),
            (g_out, act, dact, n2, middle, mlp_w, gains),
            [((rows, D), F32)] + extra,
            "mlp_bwd",
            2 * rows * D * FF * (4 if full else 2),
        )
        extra = (
            [((2, 2, 4, B, B), BF), ((2, 768), F32), ((3, D), F32), ((4, 4 * PAD, PAD), F32)]
            if full
            else []
        )
        res2 = run(
            lambda *a: attn_bwd(full, win, *a),
            (res[0], mixed, qkv, probs, normed, h, attn_w, gains),
            [((rows, D), BF)] + extra,
            "attn_bwd",
            2 * rows * D * D * 8,
            [pltpu.VMEM((rows, D), BF), pltpu.VMEM((2, rows, 768), BF)],
        )
        return res[1:], res2[1:], from_win(res2[0])

    both = ("pipe", "col")
    _, nat = forward(to_win(images))
    kept_part = lax.ppermute(nat[:, 98 - KEPT :], both, [(0, 2), (1, 3)])
    sent_part = lax.ppermute(nat[:, : 98 - KEPT], both, [(0, 3), (1, 2)])
    received = jnp.concatenate([kept_part, sent_part], axis=1)
    kept, nat_out = forward(to_win(jnp.where(first, images, received)))

    cot_swap = swap(cotangent[:, : 98 - KEPT], "col")
    cot = jnp.concatenate([cotangent[:, 98 - KEPT :], cot_swap], axis=1)
    _, _, g_nat = backward(kept, to_win(cot), False)
    g_kept = lax.ppermute(g_nat[:, :KEPT], both, [(2, 0), (3, 1)])
    g_sent = lax.ppermute(g_nat[:, KEPT:], both, [(2, 1), (3, 0)])
    g_received = jnp.concatenate([g_sent, g_kept], axis=1)
    mlp_res, attn_res, g_in = backward(kept, to_win(jnp.where(first, g_received, cot)), True)

    def unroll(x):
        back = swap(x[:, KEPT:], "col")
        return jnp.where(first, x, jnp.concatenate([back, x[:, :KEPT]], axis=1))

    layer_outputs = unroll(nat_out)[None]
    input_grads = unroll(g_in)[None]

    def reduce_grads(x):
        mine = lax.dynamic_index_in_dim(x, row, 0, keepdims=False)
        other = lax.dynamic_index_in_dim(x, 1 - row, 0, keepdims=False)
        y = mine.astype(F32) + swap(other, "row").astype(F32)
        mine = lax.dynamic_index_in_dim(y, col, 0, keepdims=False)
        other = lax.dynamic_index_in_dim(y, 1 - col, 0, keepdims=False).astype(BF)
        z = mine + swap(other, "col").astype(F32)
        return lax.psum(z.astype(BF), "dp").astype(F32)

    g_mlp = reduce_grads(mlp_res[0])
    g_attn = reduce_grads(attn_res[0])
    table_part = lax.dot_general(
        attn_res[3].reshape(HEADS, PAD * PAD),
        onehot,
        (((1,), (1,)), ((), ())),
        precision=lax.Precision.HIGHEST,
    )
    smalls = (mlp_res[1], mlp_res[2], attn_res[1], attn_res[2], table_part)
    flat = jnp.concatenate([s.reshape(-1) for s in smalls])
    flat = lax.psum(flat, ("dp", "row", "col"))
    parts, at = [], 0
    for s in smalls:
        parts.append(flat[at : at + s.size].reshape(s.shape))
        at += s.size
    b1_grad, mlp_small, qkv_small, attn_small, table_sum = parts
    pick = lambda x: lax.dynamic_index_in_dim(x, col, 0, keepdims=False)
    b1_grad = pick(b1_grad.reshape(2, 1024))
    qkv_small = pick(qkv_small).reshape(3, B)
    qkv_bias_grad = jnp.stack([qkv_small[0], qkv_small[2]], 0)
    table_grad = pick(table_sum.reshape(2, HEADS // 2, TABLE)).T
    gain_grad = jnp.stack([attn_small[0], mlp_small[0]], 0)
    offset_grad = jnp.stack([attn_small[1], mlp_small[1]], 0)
    return (
        layer_outputs,
        input_grads,
        g_attn[:3].transpose(1, 0, 2)[None],
        qkv_bias_grad[None],
        g_attn[3][None],
        attn_small[2][None],
        g_mlp[:4].transpose(1, 0, 2).reshape(B, 1024)[None],
        b1_grad[None],
        g_mlp[4:].reshape(1024, B)[None],
        mlp_small[2][None],
        gain_grad[None],
        offset_grad[None],
        table_grad[None],
    )


def solution(mesh):
    placed = (
        P(("dp", "row"), "col", None),
        P(("dp", "row"), None),
        P(("dp", "row"), "col", None),
        P("pipe", "row", None, "col"),
        P("pipe", None, "col"),
        P("pipe", "col", "row"),
        P("pipe", None),
        P("pipe", "row", "col"),
        P("pipe", "col"),
        P("pipe", "col", "row"),
        P("pipe", None),
        P("pipe", None, None),
        P("pipe", None, None),
        P("pipe", None, "col"),
    )
    return jax.shard_map(
        per_device,
        mesh=mesh,
        in_specs=placed,
        out_specs=(
            P("pipe", ("dp", "row"), "col", None),
            P("pipe", ("dp", "row"), "col", None),
            P("pipe", "row", None, "col"),
            P("pipe", None, "col"),
            P("pipe", "col", "row"),
            P("pipe", None),
            P("pipe", "row", "col"),
            P("pipe", "col"),
            P("pipe", "col", "row"),
            P("pipe", None),
            P("pipe", None, None),
            P("pipe", None, None),
            P("pipe", None, "col"),
        ),
        check_vma=False,
    )
```

```python
import jax
import jax.numpy as jnp
import numpy as np
from jax import lax
from jax.experimental import pallas as pl
from jax.experimental.pallas import tpu as pltpu
from jax.sharding import PartitionSpec as P

D = 512
HEADS = 16
FF = 2048
HEAD_DIM = 32
WINDOW = 7
CELLS = 49
SIDE = 14
SHIFT = 3
SPAN = 13
TABLE = 169
PAD = 64
HALF_ROWS = 7
KEPT = 56
B = 256
SCALE = HEAD_DIM ** (-0.5)
EPS = 1e-05
BLOCKED = -1000000000.0
BF = jnp.bfloat16
F32 = jnp.float32


def nn(a, b):
    return lax.dot_general(a, b, (((1,), (0,)), ((), ())), preferred_element_type=F32)


def nt(a, b):
    return lax.dot_general(a, b, (((1,), (1,)), ((), ())), preferred_element_type=F32)


def tn(a, b):
    return lax.dot_general(a, b, (((0,), (0,)), ((), ())), preferred_element_type=F32)


def norm_parts(values):
    mean = jnp.mean(values, -1, keepdims=True)
    centred = values - mean
    inv = lax.rsqrt(jnp.mean(centred * centred, -1, keepdims=True) + EPS)
    return centred * inv, inv


def norm_back(grad, values, gain):
    x, inv = norm_parts(values)
    s = grad * gain
    back = (s - jnp.mean(s, -1, keepdims=True) - x * jnp.mean(s * x, -1, keepdims=True)) * inv
    return back, x


def head_mask(dtype):
    lane = lax.broadcasted_iota(jnp.int32, (4 * PAD, 128), 1) // HEAD_DIM
    row = lax.broadcasted_iota(jnp.int32, (4 * PAD, 128), 0) // PAD
    return (lane == row).astype(F32).astype(dtype)


def four(x):
    return jnp.concatenate([x, x, x, x], axis=0)


def fold(x, mask):
    y = x * mask
    return y[:PAD] + y[PAD : 2 * PAD] + y[2 * PAD : 3 * PAD] + y[3 * PAD :]


def cut(j):
    return slice(j * B, (j + 1) * B)


def attn_fwd(win, h, allow, rel, w, qb, pb, gains, offs, normed, qkv, probs, mixed, middle):
    hv = h[...].astype(F32)
    x, _ = norm_parts(hv)
    nv = (x * gains[0:1] + offs[0:1]).astype(BF)
    normed[...] = nv
    for c in range(2):
        for t in range(3):
            acc = nn(nv[:, cut(0)], w[0, c, t]) + nn(nv[:, cut(1)], w[1, c, t])
            qkv[c, :, cut(t)] = (acc + qb[c : c + 1, cut(t)]).astype(BF)
    mask_low = head_mask(BF)
    mask = head_mask(F32)
    for c in range(2):
        for g in range(2):
            grp = 2 * c + g
            for n in range(win):
                rows = slice(n * PAD, (n + 1) * PAD)
                q = qkv[c, rows, g * 128 : g * 128 + 128]
                k = qkv[c, rows, B + g * 128 : B + g * 128 + 128]
                v = qkv[c, rows, 2 * B + g * 128 : 2 * B + g * 128 + 128]
                s = nt(four(q) * mask_low, k) * SCALE + rel[grp]
                s = jnp.where(allow[n] > 0.5, s, BLOCKED)
                e = jnp.exp(s - jnp.max(s, -1, keepdims=True))
                p = e / jnp.sum(e, -1, keepdims=True)
                probs[n * 4 + grp] = p
                o = fold(nn(p.astype(BF), v), mask)
                mixed[rows, grp * 128 : grp * 128 + 128] = o.astype(BF)
    mv = mixed[...]
    for r in range(2):
        acc = nn(mv[:, cut(0)], w[r, 0, 3]) + nn(mv[:, cut(1)], w[r, 1, 3])
        middle[:, cut(r)] = hv[:, cut(r)] + (acc + pb[:, cut(r)])


def mlp_fwd(middle, w, b1, b2, gains, offs, n2, act, dact, out):
    mv = middle[...]
    x, _ = norm_parts(mv)
    nv = (x * gains[1:2] + offs[1:2]).astype(BF)
    n2[...] = nv
    acc = [mv[:, cut(r)] + b2[:, cut(r)] for r in range(2)]
    for c in range(2):
        for j in range(4):
            cols = slice(c * 1024 + j * B, c * 1024 + (j + 1) * B)
            pre = nn(nv[:, cut(0)], w[0, c, j]) + nn(nv[:, cut(1)], w[1, c, j]) + b1[:, cols]
            phi = 0.5 + 0.5 * lax.erf(pre * (0.5 ** 0.5))
            av = (pre * phi).astype(BF)
            act[:, cols] = av
            dact[:, cols] = phi + pre * (jnp.exp(-0.5 * pre * pre) * 0.3989422804014327)
            for r in range(2):
                acc[r] = acc[r] + nn(av, w[r, c, 4 + j])
    for r in range(2):
        out[:, cut(r)] = acc[r].astype(BF)


def mlp_bwd(full, g_out, act, dact, n2, middle, w, gains, *outs):
    gz = g_out[...]
    gn = [None, None]
    for c in range(2):
        for j in range(4):
            cols = slice(c * 1024 + j * B, c * 1024 + (j + 1) * B)
            ga = nt(gz[:, cut(0)], w[0, c, 4 + j]) + nt(gz[:, cut(1)], w[1, c, 4 + j])
            gp = (ga * dact[:, cols]).astype(BF)
            for r in range(2):
                t = nt(gp, w[r, c, j])
                gn[r] = t if gn[r] is None else gn[r] + t
            if full:
                av = act[:, cols]
                outs[2][:, cols] = jnp.sum(gp.astype(F32), 0, keepdims=True)
                for r in range(2):
                    outs[1][r, c, 4 + j] = tn(av, gz[:, cut(r)]).astype(BF)
                    outs[1][r, c, j] = tn(n2[:, cut(r)], gp).astype(BF)
    gnv = jnp.concatenate(gn, axis=1)
    back, x = norm_back(gnv, middle[...], gains[1:2])
    gf = gz.astype(F32)
    outs[0][...] = gf + back
    if full:
        outs[3][0:1] = jnp.sum(gnv * x, 0, keepdims=True)
        outs[3][1:2] = jnp.sum(gnv, 0, keepdims=True)
        outs[3][2:3] = jnp.sum(gf, 0, keepdims=True)


def attn_bwd(full, win, gm, mixed, qkv, probs, normed, h, w, gains, *rest):
    outs, (gmix, gqkv) = rest[:-2], rest[-2:]
    gmv = gm[...]
    ga = gmv.astype(BF)
    for c in range(2):
        acc = nt(ga[:, cut(0)], w[0, c, 3]) + nt(ga[:, cut(1)], w[1, c, 3])
        gmix[:, cut(c)] = acc.astype(BF)
    mask_low = head_mask(BF)
    mask = head_mask(F32)
    for c in range(2):
        for g in range(2):
            grp = 2 * c + g
            total = None
            for n in range(win):
                rows = slice(n * PAD, (n + 1) * PAD)
                q = qkv[c, rows, g * 128 : g * 128 + 128]
                k = qkv[c, rows, B + g * 128 : B + g * 128 + 128]
                v = qkv[c, rows, 2 * B + g * 128 : 2 * B + g * 128 + 128]
                g4 = four(gmix[rows, grp * 128 : grp * 128 + 128]) * mask_low
                p = probs[n * 4 + grp]
                gp = nt(g4, v)
                ds = (p * (gp - jnp.sum(p * gp, -1, keepdims=True))).astype(BF)
                gv = tn(p.astype(BF), g4)
                gq = fold(nn(ds, k), mask) * SCALE
                gk = tn(ds, four(q) * mask_low) * SCALE
                gqkv[c, rows, g * 128 : g * 128 + 128] = gq.astype(BF)
                gqkv[c, rows, B + g * 128 : B + g * 128 + 128] = gk.astype(BF)
                gqkv[c, rows, 2 * B + g * 128 : 2 * B + g * 128 + 128] = gv.astype(BF)
                if full:
                    total = ds.astype(F32) if total is None else total + ds.astype(F32)
            if full:
                outs[4][grp] = total
    gn = [None, None]
    for c in range(2):
        for t in range(3):
            gt = gqkv[c, :, cut(t)]
            for r in range(2):
                part = nt(gt, w[r, c, t])
                gn[r] = part if gn[r] is None else gn[r] + part
                if full:
                    outs[1][r, c, t] = tn(normed[:, cut(r)], gt).astype(BF)
            if full:
                outs[2][c : c + 1, cut(t)] = jnp.sum(gt.astype(F32), 0, keepdims=True)
    gnv = jnp.concatenate(gn, axis=1)
    back, x = norm_back(gnv, h[...].astype(F32), gains[0:1])
    outs[0][...] = (gmv + back).astype(BF)
    if full:
        for c in range(2):
            for r in range(2):
                outs[1][r, c, 3] = tn(mixed[:, cut(c)], ga[:, cut(r)]).astype(BF)
        outs[3][0:1] = jnp.sum(gnv * x, 0, keepdims=True)
        outs[3][1:2] = jnp.sum(gnv, 0, keepdims=True)
        outs[3][2:3] = jnp.sum(ga.astype(F32), 0, keepdims=True)


def partner_copy(src, dst, send, recv, device):
    return pltpu.make_async_remote_copy(
        src_ref=src,
        dst_ref=dst,
        send_sem=send,
        recv_sem=recv,
        device_id=device,
        device_id_type=pl.DeviceIdType.MESH,
    )


def greet(devices):
    barrier = pltpu.get_barrier_semaphore()
    for device in devices:
        pl.semaphore_signal(barrier, inc=1, device_id=device, device_id_type=pl.DeviceIdType.MESH)
    return barrier


def first_fwd(win, h, allow, rel, la, lm, qb, pb, b1, b2, gains, offs, *rest):
    out, wa, wm, normed, qkv, probs, mixed, middle, cs, cr, rs, rr, fs, fr = rest
    row, col = lax.axis_index("row"), lax.axis_index("col")
    to_row, to_col = {"row": 1 - row}, {"col": 1 - col}
    barrier = greet([to_row, to_col])
    pl.semaphore_wait(barrier, 2)
    blocks = [(la, wa, k) for k in range(4)]
    for j in range(4):
        blocks += [(lm, wm, j), (lm, wm, 4 + j)]
    over_col, over_row, onward = [], [], []
    for i, (src, dst, k) in enumerate(blocks):
        over_col.append(
            partner_copy(src.at[k], dst.at[row, col, k], cs.at[i], cr.at[i], to_col)
        )
        over_row.append(
            partner_copy(src.at[k], dst.at[row, col, k], rs.at[i], rr.at[i], to_row)
        )
        far = dst.at[row, 1 - col, k]
        onward.append(partner_copy(far, far, fs.at[i], fr.at[i], to_row))
        over_col[i].start()
        over_row[i].start()
    wa[row, col] = la[...]
    wm[row, col] = lm[...]
    for i in range(4):
        over_col[i].wait_recv()
        onward[i].start()
    for i in range(4):
        over_row[i].wait_recv()
        onward[i].wait_recv()
    attn_fwd(win, h, allow, rel, wa, qb, pb, gains, offs, normed, qkv, probs, mixed, middle)
    mv = middle[...]
    x, _ = norm_parts(mv)
    nv = (x * gains[1:2] + offs[1:2]).astype(BF)
    acc = [mv[:, cut(r)] + b2[:, cut(r)] for r in range(2)]
    for near in range(2):
        c = col if near == 0 else 1 - col
        for j in range(4):
            for i in (4 + 2 * j, 5 + 2 * j):
                if near == 0:
                    over_row[i].wait_recv()
                else:
                    over_col[i].wait_recv()
                    onward[i].start()
            if near == 1:
                onward[4 + 2 * j].wait_recv()
                onward[5 + 2 * j].wait_recv()
            pre = nn(nv[:, cut(0)], wm[0, c, j]) + nn(nv[:, cut(1)], wm[1, c, j]) + b1[c * 4 + j]
            av = (pre * (0.5 + 0.5 * lax.erf(pre * (0.5 ** 0.5)))).astype(BF)
            for r in range(2):
                acc[r] = acc[r] + nn(av, wm[r, c, 4 + j])
    for r in range(2):
        out[:, cut(r)] = acc[r].astype(BF)
    for i in range(12):
        over_col[i].wait_send()
        over_row[i].wait_send()
        onward[i].wait_send()


def reduce_grads(line, gm, ga, out, rbuf, csend, cbuf, zsum, ebuf, wsum, mbuf, *sems):
    rs, rr, cs, cr, es, er, ms, mr, bs, br = sems
    row, col, place = lax.axis_index("row"), lax.axis_index("col"), lax.axis_index("dp")
    to_row, to_col = {"row": 1 - row}, {"col": 1 - col}
    inner = (place == 1) | (place == 2)
    outer = jnp.logical_not(inner)
    to_pair = {"dp": place + 1 - 2 * lax.rem(place, 2)}
    to_other = {"dp": 3 - place}
    barrier = greet([to_row, to_col] + ([to_pair] if line else []))
    if line:

        @pl.when(inner)
        def _():
            greet([to_other])
            pl.semaphore_wait(barrier, 4)

        @pl.when(outer)
        def _():
            pl.semaphore_wait(barrier, 3)
    else:
        pl.semaphore_wait(barrier, 2)

    def grad(k):
        return (gm, k) if k < 8 else (ga, k - 8)

    over_row, over_col = [], []
    for k in range(12):
        ref, at = grad(k)
        over_row.append(
            partner_copy(ref.at[1 - row, :, at], rbuf.at[k], rs.at[k], rr.at[k], to_row)
        )
        over_row[k].start()
    for k in range(12):
        ref, at = grad(k)
        over_row[k].wait_recv()
        other = ref[row, 1 - col, at].astype(F32) + rbuf[k, 1 - col].astype(F32)
        csend[k] = other.astype(BF)
        over_col.append(partner_copy(csend.at[k], cbuf.at[k], cs.at[k], cr.at[k], to_col))
        over_col[k].start()
    to_inner = [
        partner_copy(zsum.at[k], ebuf.at[k], es.at[k], er.at[k], to_pair) for k in range(12 if line else 0)
    ]
    across = [
        partner_copy(wsum.at[k], mbuf.at[k], ms.at[k], mr.at[k], to_other) for k in range(12 if line else 0)
    ]
    to_outer = [
        partner_copy(out.at[k], out.at[k], bs.at[k], br.at[k], to_pair) for k in range(12 if line else 0)
    ]
    for t in range(14 if line else 12):
        if t < 12:
            ref, at = grad(t)
            over_col[t].wait_recv()
            mine = ref[row, col, at].astype(F32) + rbuf[t, col].astype(F32)
            total = (mine + cbuf[t].astype(F32)).astype(BF)
            if not line:
                out[t] = total
                continue
            zsum[t] = total

            @pl.when(outer)
            def _():
                to_inner[t].start()

        @pl.when(inner)
        def _():
            if 1 <= t < 13:
                k = t - 1
                to_inner[k].wait_recv()
                wsum[k] = (zsum[k].astype(F32) + ebuf[k].astype(F32)).astype(BF)
                across[k].start()
            if t >= 2:
                k = t - 2
                across[k].wait_recv()
                out[k] = (wsum[k].astype(F32) + mbuf[k].astype(F32)).astype(BF)
                to_outer[k].start()

    for k in range(12):
        over_row[k].wait_send()
        over_col[k].wait_send()
    if line:

        @pl.when(outer)
        def _():
            for k in range(12):
                to_outer[k].wait_recv()
                to_inner[k].wait_send()

        @pl.when(inner)
        def _():
            for k in range(12):
                across[k].wait_send()
                to_outer[k].wait_send()


def run(body, args, outs, name, flops, scratch=(), shared=None):
    shapes = [jax.ShapeDtypeStruct(s, d) for s, d in outs]
    moved = sum(a.size * a.dtype.itemsize for a in list(args) + shapes)
    vm = pl.BlockSpec(memory_space=pltpu.VMEM)
    return pl.pallas_call(
        body,
        out_shape=shapes,
        in_specs=[vm] * len(args),
        out_specs=[vm] * len(outs),
        scratch_shapes=list(scratch),
        compiler_params=pltpu.CompilerParams(
            vmem_limit_bytes=48 * 1024 * 1024,
            collective_id=shared,
            has_side_effects=shared is not None,
        ),
        cost_estimate=pl.CostEstimate(flops=flops, bytes_accessed=moved, transcendentals=0),
        name=name,
    )(*args)


def place_matrix(images, shift):
    out = np.zeros((images * 2 * PAD, images * 98), np.float32)
    for n in range(images):
        for r in range(HALF_ROWS):
            for c in range(SIDE):
                rolled = (c - shift) % SIDE
                row = (n * 2 + rolled // WINDOW) * PAD + r * WINDOW + rolled % WINDOW
                out[row, n * 98 + r * SIDE + c] = 1.0
    return out


def allowed_cells(extents, section, col):
    images = extents.shape[0]
    places = jnp.arange(SIDE, dtype=jnp.int32)
    source = (places + SHIFT * section) % SIDE
    padded = (source[None, :, None] >= extents[:, 0, None, None]) | (
        source[None, None, :] >= extents[:, 1, None, None]
    )
    band = (places >= SIDE - WINDOW).astype(jnp.int32) + (places >= SIDE - SHIFT).astype(jnp.int32)
    codes = (band[:, None] * 3 + band[None, :]) * section * 2 + padded.astype(jnp.int32)
    mine = lax.dynamic_slice_in_dim(codes, col * HALF_ROWS, HALF_ROWS, 1)
    mine = mine.reshape(images, HALF_ROWS, 2, WINDOW).transpose(0, 2, 1, 3)
    mine = mine.reshape(images * 2, CELLS)
    query = jnp.pad(mine, ((0, 0), (0, PAD - CELLS)))
    key = jnp.pad(mine, ((0, 0), (0, PAD - CELLS)), constant_values=-1)
    real = jnp.arange(PAD) < CELLS
    same = (query[:, :, None] == key[:, None, :]) | ((~real)[None, :, None] & real[None, None, :])
    return jnp.tile(same.astype(F32), (1, 4, 1))


def relative_onehot():
    cells = np.arange(CELLS)
    a, b = cells // WINDOW, cells % WINDOW
    index = (a[:, None] - a[None, :] + WINDOW - 1) * SPAN + b[:, None] - b[None, :] + WINDOW - 1
    full = np.full((PAD, PAD), -1, np.int32)
    full[:CELLS, :CELLS] = index
    return jnp.asarray(full.reshape(-1))[None, :] == jnp.arange(TABLE, dtype=jnp.int32)[:, None]


def per_device(
    images,
    extents,
    cotangent,
    qkv_weight,
    qkv_bias,
    proj_weight,
    proj_bias,
    fc1_weight,
    fc1_bias,
    fc2_weight,
    fc2_bias,
    norm_gain,
    norm_bias,
    bias_table,
):
    section = lax.axis_index("pipe")
    row = lax.axis_index("row")
    col = lax.axis_index("col")
    first = section == 0
    count = images.shape[0]
    win = count * 2
    rows = win * PAD

    def swap(x, axis):
        return lax.ppermute(x, axis, [(0, 1), (1, 0)])

    attn_w = jnp.concatenate(
        [qkv_weight[0].transpose(1, 0, 2), proj_weight], axis=0
    )
    mlp_w = jnp.concatenate(
        [fc1_weight[0].reshape(B, 4, B).transpose(1, 0, 2), fc2_weight[0].reshape(4, B, B)], axis=0
    )

    zeros = jnp.zeros_like(qkv_bias[0, 0])
    packed = jnp.concatenate(
        [qkv_bias[0, 0], zeros, qkv_bias[0, 1], fc1_bias[0], bias_table[0].T.reshape(-1)]
    )
    packed_other = swap(packed, "col")
    packed = jnp.where(
        col == 0, jnp.stack([packed, packed_other]), jnp.stack([packed_other, packed])
    )
    qb = packed[:, :768]
    b1 = packed[:, 768:1792].reshape(1, FF)
    table = packed[:, 1792:].reshape(HEADS, TABLE)
    pb, b2, gains, offs = proj_bias, fc2_bias, norm_gain[0], norm_bias[0]
    onehot = relative_onehot().astype(F32)
    rel = jnp.dot(table, onehot, precision=lax.Precision.HIGHEST).reshape(4, 4 * PAD, PAD)
    allow = allowed_cells(extents, section, col)
    place = jnp.where(
        first, jnp.asarray(place_matrix(count, 0), BF), jnp.asarray(place_matrix(count, SHIFT), BF)
    )

    def to_win(nat):
        return nn(place, nat.reshape(count * 98, D)).astype(BF)

    def from_win(x):
        return tn(place, x).astype(BF).reshape(count, 98, D)

    def forward(h):
        normed, qkv, probs, mixed, middle = run(
            lambda *a: attn_fwd(win, *a),
            (h, allow, rel, attn_w, qb, pb, gains, offs),
            [
                ((rows, D), BF),
                ((2, rows, 768), BF),
                ((win * 4, 4 * PAD, PAD), F32),
                ((rows, D), BF),
                ((rows, D), F32),
            ],
            "attn_fwd",
            2 * rows * D * D * 4,
        )
        n2, act, dact, out = run(
            mlp_fwd,
            (middle, mlp_w, b1, b2, gains, offs),
            [((rows, D), BF), ((rows, FF), BF), ((rows, FF), F32), ((rows, D), BF)],
            "mlp_fwd",
            2 * rows * D * FF * 2,
        )
        return (h, normed, qkv, probs, mixed, middle, n2, act, dact), from_win(out)

    def backward(kept, g_out, full):
        h, normed, qkv, probs, mixed, middle, n2, act, dact = kept
        extra = [((2, 2, 8, B, B), BF), ((1, FF), F32), ((3, D), F32)] if full else []
        res = run(
            lambda *a: mlp_bwd(full, *a),
            (g_out, act, dact, n2, middle, mlp_w, gains),
            [((rows, D), F32)] + extra,
            "mlp_bwd",
            2 * rows * D * FF * (4 if full else 2),
        )
        extra = (
            [((2, 2, 4, B, B), BF), ((2, 768), F32), ((3, D), F32), ((4, 4 * PAD, PAD), F32)]
            if full
            else []
        )
        res2 = run(
            lambda *a: attn_bwd(full, win, *a),
            (res[0], mixed, qkv, probs, normed, h, attn_w, gains),
            [((rows, D), BF)] + extra,
            "attn_bwd",
            2 * rows * D * D * 8,
            [pltpu.VMEM((rows, D), BF), pltpu.VMEM((2, rows, 768), BF)],
        )
        return res[1:], res2[1:], from_win(res2[0])

    both = ("pipe", "col")
    dma = pltpu.SemaphoreType.DMA((12,))
    out_first, attn_w, mlp_w = run(
        lambda *a: first_fwd(win, *a),
        (
            to_win(images),
            allow,
            rel,
            attn_w,
            mlp_w,
            qb,
            pb,
            b1.reshape(8, 1, B),
            b2,
            gains,
            offs,
        ),
        [((rows, D), BF), ((2, 2, 4, B, B), BF), ((2, 2, 8, B, B), BF)],
        "first_fwd",
        2 * rows * D * (4 * D + 2 * FF),
        [
            pltpu.VMEM((rows, D), BF),
            pltpu.VMEM((2, rows, 768), BF),
            pltpu.VMEM((win * 4, 4 * PAD, PAD), F32),
            pltpu.VMEM((rows, D), BF),
            pltpu.VMEM((rows, D), F32),
        ]
        + [dma] * 6,
        0,
    )
    nat = from_win(out_first)
    kept_part = lax.ppermute(nat[:, 98 - KEPT :], both, [(0, 2), (1, 3)])
    sent_part = lax.ppermute(nat[:, : 98 - KEPT], both, [(0, 3), (1, 2)])
    received = jnp.concatenate([kept_part, sent_part], axis=1)
    kept, nat_out = forward(to_win(jnp.where(first, images, received)))

    cot_swap = swap(cotangent[:, : 98 - KEPT], "col")
    cot = jnp.concatenate([cotangent[:, 98 - KEPT :], cot_swap], axis=1)
    _, _, g_nat = backward(kept, to_win(cot), False)
    g_kept = lax.ppermute(g_nat[:, :KEPT], both, [(2, 0), (3, 1)])
    g_sent = lax.ppermute(g_nat[:, KEPT:], both, [(2, 1), (3, 0)])
    g_received = jnp.concatenate([g_sent, g_kept], axis=1)
    mlp_res, attn_res, g_in = backward(kept, to_win(jnp.where(first, g_received, cot)), True)

    def unroll(x):
        back = swap(x[:, KEPT:], "col")
        return jnp.where(first, x, jnp.concatenate([back, x[:, :KEPT]], axis=1))

    layer_outputs = unroll(nat_out)[None]
    input_grads = unroll(g_in)[None]

    line = lax.axis_size("dp") == 4
    block = pltpu.VMEM((12, B, B), BF)
    (grads,) = run(
        lambda *a: reduce_grads(line, *a),
        (mlp_res[0], attn_res[0]),
        [((12, B, B), BF)],
        "reduce_grads",
        12 * B * B * 16,
        [pltpu.VMEM((12, 2, B, B), BF)] + [block] * 6 + [dma] * 10,
        1,
    )
    if not line:
        grads = lax.psum(grads, "dp")
    grads = grads.astype(F32)
    g_mlp, g_attn = grads[:8], grads[8:]
    table_part = lax.dot_general(
        attn_res[3].reshape(HEADS, PAD * PAD),
        onehot,
        (((1,), (1,)), ((), ())),
        precision=lax.Precision.HIGHEST,
    )
    smalls = (mlp_res[1], mlp_res[2], attn_res[1], attn_res[2], table_part)
    flat = jnp.concatenate([s.reshape(-1) for s in smalls])
    flat = lax.psum(flat, ("dp", "row", "col"))
    parts, at = [], 0
    for s in smalls:
        parts.append(flat[at : at + s.size].reshape(s.shape))
        at += s.size
    b1_grad, mlp_small, qkv_small, attn_small, table_sum = parts
    pick = lambda x: lax.dynamic_index_in_dim(x, col, 0, keepdims=False)
    b1_grad = pick(b1_grad.reshape(2, 1024))
    qkv_small = pick(qkv_small).reshape(3, B)
    qkv_bias_grad = jnp.stack([qkv_small[0], qkv_small[2]], 0)
    table_grad = pick(table_sum.reshape(2, HEADS // 2, TABLE)).T
    gain_grad = jnp.stack([attn_small[0], mlp_small[0]], 0)
    offset_grad = jnp.stack([attn_small[1], mlp_small[1]], 0)
    return (
        layer_outputs,
        input_grads,
        g_attn[:3].transpose(1, 0, 2)[None],
        qkv_bias_grad[None],
        g_attn[3][None],
        attn_small[2][None],
        g_mlp[:4].transpose(1, 0, 2).reshape(B, 1024)[None],
        b1_grad[None],
        g_mlp[4:].reshape(1024, B)[None],
        mlp_small[2][None],
        gain_grad[None],
        offset_grad[None],
        table_grad[None],
    )


def solution(mesh):
    placed = (
        P(("dp", "row"), "col", None),
        P(("dp", "row"), None),
        P(("dp", "row"), "col", None),
        P("pipe", "row", None, "col"),
        P("pipe", None, "col"),
        P("pipe", "col", "row"),
        P("pipe", None),
        P("pipe", "row", "col"),
        P("pipe", "col"),
        P("pipe", "col", "row"),
        P("pipe", None),
        P("pipe", None, None),
        P("pipe", None, None),
        P("pipe", None, "col"),
    )
    return jax.shard_map(
        per_device,
        mesh=mesh,
        in_specs=placed,
        out_specs=(
            P("pipe", ("dp", "row"), "col", None),
            P("pipe", ("dp", "row"), "col", None),
            P("pipe", "row", None, "col"),
            P("pipe", None, "col"),
            P("pipe", "col", "row"),
            P("pipe", None),
            P("pipe", "row", "col"),
            P("pipe", "col"),
            P("pipe", "col", "row"),
            P("pipe", None),
            P("pipe", None, None),
            P("pipe", None, None),
            P("pipe", None, "col"),
        ),
        check_vma=False,
    )
```

```python
import jax
import jax.numpy as jnp
import numpy as np
from jax import lax
from jax.experimental import pallas as pl
from jax.experimental.pallas import tpu as pltpu
from jax.sharding import PartitionSpec as P

D = 512
HEADS = 16
FF = 2048
HEAD_DIM = 32
WINDOW = 7
CELLS = 49
SIDE = 14
SHIFT = 3
SPAN = 13
TABLE = 169
PAD = 64
HALF_ROWS = 7
KEPT = 56
KEEP = 112
SENT = 96
B = 256
SCALE = HEAD_DIM ** (-0.5)
EPS = 1e-05
BLOCKED = -1000000000.0
BF = jnp.bfloat16
F32 = jnp.float32


def nn(a, b):
    return lax.dot_general(a, b, (((1,), (0,)), ((), ())), preferred_element_type=F32)


def nt(a, b):
    return lax.dot_general(a, b, (((1,), (1,)), ((), ())), preferred_element_type=F32)


def tn(a, b):
    return lax.dot_general(a, b, (((0,), (0,)), ((), ())), preferred_element_type=F32)


def norm_parts(values):
    mean = jnp.mean(values, -1, keepdims=True)
    centred = values - mean
    inv = lax.rsqrt(jnp.mean(centred * centred, -1, keepdims=True) + EPS)
    return centred * inv, inv


def norm_back(grad, values, gain):
    x, inv = norm_parts(values)
    s = grad * gain
    back = (s - jnp.mean(s, -1, keepdims=True) - x * jnp.mean(s * x, -1, keepdims=True)) * inv
    return back, x


def head_mask(dtype):
    lane = lax.broadcasted_iota(jnp.int32, (4 * PAD, 128), 1) // HEAD_DIM
    row = lax.broadcasted_iota(jnp.int32, (4 * PAD, 128), 0) // PAD
    return (lane == row).astype(F32).astype(dtype)


def four(x):
    return jnp.concatenate([x, x, x, x], axis=0)


def fold(x, mask):
    y = x * mask
    return y[:PAD] + y[PAD : 2 * PAD] + y[2 * PAD : 3 * PAD] + y[3 * PAD :]


def cut(j):
    return slice(j * B, (j + 1) * B)


def attn_fwd(win, h, allow, rel, w, qb, pb, gains, offs, normed, qkv, probs, mixed, middle):
    hv = h[...].astype(F32)
    x, _ = norm_parts(hv)
    nv = (x * gains[0:1] + offs[0:1]).astype(BF)
    normed[...] = nv
    for c in range(2):
        for t in range(3):
            acc = nn(nv[:, cut(0)], w[0, c, t]) + nn(nv[:, cut(1)], w[1, c, t])
            qkv[c, :, cut(t)] = (acc + qb[c : c + 1, cut(t)]).astype(BF)
    mask_low = head_mask(BF)
    mask = head_mask(F32)
    for c in range(2):
        for g in range(2):
            grp = 2 * c + g
            for n in range(win):
                rows = slice(n * PAD, (n + 1) * PAD)
                q = qkv[c, rows, g * 128 : g * 128 + 128]
                k = qkv[c, rows, B + g * 128 : B + g * 128 + 128]
                v = qkv[c, rows, 2 * B + g * 128 : 2 * B + g * 128 + 128]
                s = nt(four(q) * mask_low, k) * SCALE + rel[grp]
                s = jnp.where(allow[n] > 0.5, s, BLOCKED)
                e = jnp.exp(s - jnp.max(s, -1, keepdims=True))
                p = e / jnp.sum(e, -1, keepdims=True)
                probs[n * 4 + grp] = p
                o = fold(nn(p.astype(BF), v), mask)
                mixed[rows, grp * 128 : grp * 128 + 128] = o.astype(BF)
    mv = mixed[...]
    for r in range(2):
        acc = nn(mv[:, cut(0)], w[r, 0, 3]) + nn(mv[:, cut(1)], w[r, 1, 3])
        middle[:, cut(r)] = hv[:, cut(r)] + (acc + pb[:, cut(r)])


def partner_copy(src, dst, send, recv, device):
    return pltpu.make_async_remote_copy(
        src_ref=src,
        dst_ref=dst,
        send_sem=send,
        recv_sem=recv,
        device_id=device,
        device_id_type=pl.DeviceIdType.MESH,
    )


def greet(devices):
    barrier = pltpu.get_barrier_semaphore()
    for device in devices:
        pl.semaphore_signal(barrier, inc=1, device_id=device, device_id_type=pl.DeviceIdType.MESH)
    return barrier


def whole_step(win, line, *refs):
    (img, cot, place, allow, rel, la, lm, qb, pb, b1, b2, gains, offs) = refs[:13]
    (out_k, out_s, gin_k, gin_s, grads, small_out, table_out) = refs[13:20]
    (wa, wm, normed, qkv, probs, mixed, middle, h, n2, act, dact, gpre, gz, gm, ga) = refs[20:35]
    (gmix, gqkv, grid, back, hop, cot_in, out_in, gin_in) = refs[35:43]
    (gbuf, rbuf, csend, cbuf, zsum, ebuf, wsum, mbuf) = refs[43:51]
    (small, table, hold_f, hold_b) = refs[51:55]
    (cs, cr, rs, rr, fs, fr, hs, hr) = refs[55:63]
    (rs2, rr2, cs2, cr2, es, er, ms, mr, bs, br, ps, pr) = refs[63:75]
    section = lax.axis_index("pipe")
    row, col, spot = lax.axis_index("row"), lax.axis_index("col"), lax.axis_index("dp")
    first, second = section == 0, section == 1
    to_row, to_col = {"row": 1 - row}, {"col": 1 - col}
    to_next, to_cross = {"pipe": 1 - section}, {"pipe": 1 - section, "col": 1 - col}
    inner = (spot == 1) | (spot == 2)
    outer = jnp.logical_not(inner)
    to_pair = {"dp": spot + 1 - 2 * lax.rem(spot, 2)}
    to_other = {"dp": 3 - spot}
    barrier = greet([to_row, to_col, to_next, to_cross] + ([to_pair] if line else []))
    if line:

        @pl.when(inner)
        def _():
            greet([to_other])
            pl.semaphore_wait(barrier, 6)

        @pl.when(outer)
        def _():
            pl.semaphore_wait(barrier, 5)
    else:
        pl.semaphore_wait(barrier, 4)

    blocks = [(la, wa, k) for k in range(4)]
    for j in range(4):
        blocks += [(lm, wm, j), (lm, wm, 4 + j)]
    over_col, over_row, onward = [], [], []
    for i, (src, dst, k) in enumerate(blocks):
        over_col.append(
            partner_copy(src.at[k], dst.at[row, col, k], cs.at[i], cr.at[i], to_col)
        )
        over_row.append(
            partner_copy(src.at[k], dst.at[row, col, k], rs.at[i], rr.at[i], to_row)
        )
        far = dst.at[row, 1 - col, k]
        onward.append(partner_copy(far, far, fs.at[i], fr.at[i], to_row))
        over_col[i].start()
        over_row[i].start()
    cot_copy = partner_copy(cot.at[pl.ds(KEEP, SENT)], cot_in, hs.at[2], hr.at[2], to_col)
    cot_copy.start()
    wa[row, col] = la[...]
    wm[row, col] = lm[...]
    hop_keep = partner_copy(
        grid.at[pl.ds(0, KEEP)], hop.at[pl.ds(0, KEEP)], hs.at[0], hr.at[0], to_next
    )
    hop_cross = partner_copy(
        grid.at[pl.ds(KEEP, SENT)], hop.at[pl.ds(KEEP, SENT)], hs.at[1], hr.at[1], to_cross
    )
    for i in range(4):
        over_col[i].wait_recv()
        onward[i].start()
    for i in range(4):
        over_row[i].wait_recv()
        onward[i].wait_recv()

    @pl.when(first)
    def _():
        h[...] = nn(place[...], img[...]).astype(BF)

    @pl.when(second)
    def _():
        for i in range(4, 12):
            over_col[i].wait_recv()
            onward[i].start()
        hop_keep.wait_recv()
        hop_cross.wait_recv()
        h[...] = nn(place[...], hop[...]).astype(BF)

    attn_fwd(win, h, allow, rel, wa, qb, pb, gains, offs, normed, qkv, probs, mixed, middle)
    mv = middle[...]
    x, _ = norm_parts(mv)
    nv = (x * gains[1:2] + offs[1:2]).astype(BF)
    n2[...] = nv
    acc = [mv[:, cut(r)] + b2[:, cut(r)] for r in range(2)]
    for near in range(2):
        c = col if near == 0 else 1 - col
        for j in range(4):
            pair = (4 + 2 * j, 5 + 2 * j)
            if near == 0:
                for i in pair:
                    over_row[i].wait_recv()
            else:

                @pl.when(first)
                def _():
                    for i in pair:
                        over_col[i].wait_recv()
                        onward[i].start()

                for i in pair:
                    onward[i].wait_recv()
            at = c * 4 + j
            pre = nn(nv[:, cut(0)], wm[0, c, j]) + nn(nv[:, cut(1)], wm[1, c, j]) + b1[at]
            phi = 0.5 + 0.5 * lax.erf(pre * (0.5 ** 0.5))
            av = (pre * phi).astype(BF)
            act[at] = av
            dact[at] = phi + pre * (jnp.exp(-0.5 * pre * pre) * 0.3989422804014327)
            for r in range(2):
                acc[r] = acc[r] + nn(av, wm[r, c, 4 + j])
    outv = jnp.concatenate([acc[0].astype(BF), acc[1].astype(BF)], axis=1)
    grid[...] = tn(place[...], outv).astype(BF)
    out_copy = partner_copy(grid.at[pl.ds(KEEP, SENT)], out_in, hs.at[3], hr.at[3], to_col)

    @pl.when(first)
    def _():
        hop_keep.start()
        hop_cross.start()

    out_copy.start()
    out_k[...] = grid[:KEEP]
    out_s[...] = grid[KEEP:]
    cot_copy.wait_recv()

    @pl.when(first)
    def _():
        hop_keep.wait_recv()
        hop_cross.wait_recv()
        gz[...] = nn(place[...], hop[...]).astype(BF)

    @pl.when(second)
    def _():
        back[:KEEP] = cot[:KEEP]
        back[KEEP:] = cot_in[...]
        gz[...] = nn(place[...], back[...]).astype(BF)

    zv = gz[...]
    gn = [None, None]
    small[...] = jnp.zeros_like(small)
    for c in range(2):
        for j in range(4):
            at = c * 4 + j
            gact = nt(zv[:, cut(0)], wm[0, c, 4 + j]) + nt(zv[:, cut(1)], wm[1, c, 4 + j])
            gp = (gact * dact[at]).astype(BF)
            gpre[at] = gp
            small[0, 3 + at // 2 : 4 + at // 2, cut(at % 2)] = jnp.sum(
                gp.astype(F32), 0, keepdims=True
            )
            for r in range(2):
                t = nt(gp, wm[r, c, j])
                gn[r] = t if gn[r] is None else gn[r] + t
    gnv = jnp.concatenate(gn, axis=1)
    inv_back, x = norm_back(gnv, middle[...], gains[1:2])
    gf = zv.astype(F32)
    gm[...] = gf + inv_back
    small[0, 0:1] = jnp.sum(gnv * x, 0, keepdims=True)
    small[0, 1:2] = jnp.sum(gnv, 0, keepdims=True)
    small[0, 2:3] = jnp.sum(gf, 0, keepdims=True)

    row_copies = [
        partner_copy(gbuf.at[1 - row, :, k], rbuf.at[k], rs2.at[k], rr2.at[k], to_row)
        for k in range(12)
    ]
    col_copies = [
        partner_copy(csend.at[k], cbuf.at[k], cs2.at[k], cr2.at[k], to_col) for k in range(12)
    ]

    def mlp_grads():
        for j in range(4):
            for r in range(2):
                for c in range(2):
                    gbuf[r, c, j] = tn(n2[:, cut(r)], gpre[c * 4 + j]).astype(BF)
                    gbuf[r, c, 4 + j] = tn(act[c * 4 + j], gz[:, cut(r)]).astype(BF)
            row_copies[j].start()
            row_copies[4 + j].start()

    def pass_on(ks):
        for k in ks:
            row_copies[k].wait_recv()
            other = gbuf[row, 1 - col, k].astype(F32) + rbuf[k, 1 - col].astype(F32)
            csend[k] = other.astype(BF)
            col_copies[k].start()

    order = (0, 4, 1, 5, 2, 6, 3, 7, 8, 9, 10, 11)

    @pl.when(first)
    def _():
        mlp_grads()

    ga[...] = gm[...].astype(BF)
    for c in range(2):
        part = nt(ga[:, cut(0)], wa[0, c, 3]) + nt(ga[:, cut(1)], wa[1, c, 3])
        gmix[:, cut(c)] = part.astype(BF)
    mask_low = head_mask(BF)
    mask = head_mask(F32)
    for c in range(2):
        tables = []
        for g in range(2):
            grp = 2 * c + g
            total = None
            for n in range(win):
                rows = slice(n * PAD, (n + 1) * PAD)
                q = qkv[c, rows, g * 128 : g * 128 + 128]
                k = qkv[c, rows, B + g * 128 : B + g * 128 + 128]
                v = qkv[c, rows, 2 * B + g * 128 : 2 * B + g * 128 + 128]
                g4 = four(gmix[rows, grp * 128 : grp * 128 + 128]) * mask_low
                p = probs[n * 4 + grp]
                gp = nt(g4, v)
                ds = (p * (gp - jnp.sum(p * gp, -1, keepdims=True))).astype(BF)
                gv = tn(p.astype(BF), g4)
                gq = fold(nn(ds, k), mask) * SCALE
                gk = tn(ds, four(q) * mask_low) * SCALE
                gqkv[c, rows, g * 128 : g * 128 + 128] = gq.astype(BF)
                gqkv[c, rows, B + g * 128 : B + g * 128 + 128] = gk.astype(BF)
                gqkv[c, rows, 2 * B + g * 128 : 2 * B + g * 128 + 128] = gv.astype(BF)
                total = ds.astype(F32) if total is None else total + ds.astype(F32)
            tables.append(total)
        table[c] = jnp.concatenate(tables, axis=1).astype(BF)
        if c == 0:

            @pl.when(first)
            def _():
                pass_on(order[:8])

    gn = [None, None]
    for c in range(2):
        for t in range(3):
            gt = gqkv[c, :, cut(t)]
            at = c * 3 + t
            small[1, 3 + at // 2 : 4 + at // 2, cut(at % 2)] = jnp.sum(
                gt.astype(F32), 0, keepdims=True
            )
            for r in range(2):
                part = nt(gt, wa[r, c, t])
                gn[r] = part if gn[r] is None else gn[r] + part
    gnv = jnp.concatenate(gn, axis=1)
    inv_back, x = norm_back(gnv, h[...].astype(F32), gains[0:1])
    gin = (gm[...] + inv_back).astype(BF)
    small[1, 0:1] = jnp.sum(gnv * x, 0, keepdims=True)
    small[1, 1:2] = jnp.sum(gnv, 0, keepdims=True)
    small[1, 2:3] = jnp.sum(ga[...].astype(F32), 0, keepdims=True)

    @pl.when(first)
    def _():
        hop_keep.wait_send()
        hop_cross.wait_send()

    out_copy.wait_send()
    grid[...] = tn(place[...], gin).astype(BF)

    @pl.when(second)
    def _():
        hop_keep.start()
        hop_cross.start()

    gin_copy = partner_copy(grid.at[pl.ds(KEEP, SENT)], gin_in, hs.at[4], hr.at[4], to_col)
    gin_copy.start()
    gin_k[...] = grid[:KEEP]
    gin_s[...] = grid[KEEP:]

    def shared_copies(own, hold, final, i):
        def copy(src, dst, step, device):
            return partner_copy(src, dst, ps.at[i, step], pr.at[i, step], device)

        return [
            copy(own, hold.at[0], 0, to_row),
            copy(hold.at[1], hold.at[2], 1, to_col),
            copy(hold.at[3], hold.at[4], 2, to_pair),
            copy(hold.at[5], hold.at[6], 3, to_other),
            copy(final, final, 4, to_pair),
        ][: 5 if line else 2]

    shared = [
        (small, hold_f, small_out, shared_copies(small, hold_f, small_out, 0)),
        (table, hold_b, table_out, shared_copies(table, hold_b, table_out, 1)),
    ]

    def plus(a, b, kind):
        return (a.astype(F32) + b.astype(F32)).astype(kind)

    for own, hold, final, copies in shared:
        copies[0].start()

    @pl.when(second)
    def _():
        mlp_grads()

    for r in range(2):
        for c in range(2):
            gbuf[r, c, 11] = tn(mixed[:, cut(c)], ga[:, cut(r)]).astype(BF)
    row_copies[11].start()
    for t in range(3):
        for r in range(2):
            for c in range(2):
                gbuf[r, c, 8 + t] = tn(normed[:, cut(r)], gqkv[c, :, cut(t)]).astype(BF)
        row_copies[8 + t].start()

    @pl.when(second)
    def _():
        pass_on(order[:8])

    for own, hold, final, copies in shared:
        copies[0].wait_recv()
        hold[1] = plus(own[...], hold[0], hold.dtype)
        copies[1].start()
    pass_on(order[8:])

    to_inner = [partner_copy(zsum.at[k], ebuf.at[k], es.at[k], er.at[k], to_pair) for k in order]
    across = [partner_copy(wsum.at[k], mbuf.at[k], ms.at[k], mr.at[k], to_other) for k in order]
    to_outer = [partner_copy(grads.at[k], grads.at[k], bs.at[k], br.at[k], to_pair) for k in order]
    for t in range(15 if line else 13):
        if t < 12:
            k = order[t]
            col_copies[k].wait_recv()
            mine = gbuf[row, col, k].astype(F32) + rbuf[k, col].astype(F32)
            total = (mine + cbuf[k].astype(F32)).astype(BF)
            if line:
                zsum[k] = total

                @pl.when(outer)
                def _():
                    to_inner[t].start()
            else:
                grads[k] = total
        if t == 12:
            for own, hold, final, copies in shared:
                copies[1].wait_recv()
                total = plus(hold[1], hold[2], hold.dtype)
                if line:
                    hold[3] = total

                    @pl.when(outer)
                    def _():
                        copies[2].start()
                else:
                    final[...] = total
        if not line:
            continue

        @pl.when(inner)
        def _():
            if 1 <= t < 13:
                k = order[t - 1]
                to_inner[t - 1].wait_recv()
                wsum[k] = plus(zsum[k], ebuf[k], BF)
                across[t - 1].start()
            if t == 13:
                for own, hold, final, copies in shared:
                    copies[2].wait_recv()
                    hold[5] = plus(hold[3], hold[4], hold.dtype)
                    copies[3].start()
            if 2 <= t < 14:
                k = order[t - 2]
                across[t - 2].wait_recv()
                grads[k] = plus(wsum[k], mbuf[k], BF)
                to_outer[t - 2].start()
            if t == 14:
                for own, hold, final, copies in shared:
                    copies[3].wait_recv()
                    final[...] = plus(hold[5], hold[6], hold.dtype)
                    copies[4].start()

    out_copy.wait_recv()
    gin_copy.wait_recv()

    @pl.when(second)
    def _():
        out_s[...] = out_in[...]
        gin_s[...] = gin_in[...]
        hop_keep.wait_send()
        hop_cross.wait_send()

    gin_copy.wait_send()
    cot_copy.wait_send()
    for i in range(12):
        over_col[i].wait_send()
        over_row[i].wait_send()
        onward[i].wait_send()
        row_copies[i].wait_send()
        col_copies[i].wait_send()
    for own, hold, final, copies in shared:
        copies[0].wait_send()
        copies[1].wait_send()
    if line:

        @pl.when(outer)
        def _():
            for i in range(12):
                to_outer[i].wait_recv()
                to_inner[i].wait_send()
            for own, hold, final, copies in shared:
                copies[4].wait_recv()
                copies[2].wait_send()

        @pl.when(inner)
        def _():
            for i in range(12):
                across[i].wait_send()
                to_outer[i].wait_send()
            for own, hold, final, copies in shared:
                copies[3].wait_send()
                copies[4].wait_send()


def run(body, args, outs, name, flops, scratch=(), shared=None):
    shapes = [jax.ShapeDtypeStruct(s, d) for s, d in outs]
    moved = sum(a.size * a.dtype.itemsize for a in list(args) + shapes)
    vm = pl.BlockSpec(memory_space=pltpu.VMEM)
    return pl.pallas_call(
        body,
        out_shape=shapes,
        in_specs=[vm] * len(args),
        out_specs=[vm] * len(outs),
        scratch_shapes=list(scratch),
        compiler_params=pltpu.CompilerParams(
            vmem_limit_bytes=56 * 1024 * 1024,
            collective_id=shared,
            has_side_effects=shared is not None,
        ),
        cost_estimate=pl.CostEstimate(flops=flops, bytes_accessed=moved, transcendentals=0),
        name=name,
    )(*args)


def place_matrix(images, shift):
    out = np.zeros((images * 2 * PAD, KEEP + SENT), np.float32)
    for n in range(images):
        for r in range(HALF_ROWS):
            kept = r < 4 if shift else r >= SHIFT
            for c in range(SIDE):
                rolled = (c - shift) % SIDE
                row = (n * 2 + rolled // WINDOW) * PAD + r * WINDOW + rolled % WINDOW
                if kept:
                    at = n * 56 + (r if shift else r - SHIFT) * SIDE + c
                else:
                    at = KEEP + n * 42 + (r - 4 if shift else r) * SIDE + c
                out[row, at] = 1.0
    return out


def allowed_cells(extents, section, col):
    images = extents.shape[0]
    places = jnp.arange(SIDE, dtype=jnp.int32)
    source = (places + SHIFT * section) % SIDE
    padded = (source[None, :, None] >= extents[:, 0, None, None]) | (
        source[None, None, :] >= extents[:, 1, None, None]
    )
    band = (places >= SIDE - WINDOW).astype(jnp.int32) + (places >= SIDE - SHIFT).astype(jnp.int32)
    codes = (band[:, None] * 3 + band[None, :]) * section * 2 + padded.astype(jnp.int32)
    mine = lax.dynamic_slice_in_dim(codes, col * HALF_ROWS, HALF_ROWS, 1)
    mine = mine.reshape(images, HALF_ROWS, 2, WINDOW).transpose(0, 2, 1, 3)
    mine = mine.reshape(images * 2, CELLS)
    query = jnp.pad(mine, ((0, 0), (0, PAD - CELLS)))
    key = jnp.pad(mine, ((0, 0), (0, PAD - CELLS)), constant_values=-1)
    real = jnp.arange(PAD) < CELLS
    same = (query[:, :, None] == key[:, None, :]) | ((~real)[None, :, None] & real[None, None, :])
    return jnp.tile(same.astype(F32), (1, 4, 1))


def relative_onehot():
    cells = np.arange(CELLS)
    a, b = cells // WINDOW, cells % WINDOW
    index = (a[:, None] - a[None, :] + WINDOW - 1) * SPAN + b[:, None] - b[None, :] + WINDOW - 1
    full = np.full((PAD, PAD), -1, np.int32)
    full[:CELLS, :CELLS] = index
    return jnp.asarray(full.reshape(-1))[None, :] == jnp.arange(TABLE, dtype=jnp.int32)[:, None]


def per_device(
    images,
    extents,
    cotangent,
    qkv_weight,
    qkv_bias,
    proj_weight,
    proj_bias,
    fc1_weight,
    fc1_bias,
    fc2_weight,
    fc2_bias,
    norm_gain,
    norm_bias,
    bias_table,
):
    section = lax.axis_index("pipe")
    row = lax.axis_index("row")
    col = lax.axis_index("col")
    first = section == 0
    count = images.shape[0]
    win = count * 2
    rows = win * PAD

    def swap(x, axis):
        return lax.ppermute(x, axis, [(0, 1), (1, 0)])

    attn_w = jnp.concatenate(
        [qkv_weight[0].transpose(1, 0, 2), proj_weight], axis=0
    )
    mlp_w = jnp.concatenate(
        [fc1_weight[0].reshape(B, 4, B).transpose(1, 0, 2), fc2_weight[0].reshape(4, B, B)], axis=0
    )

    zeros = jnp.zeros_like(qkv_bias[0, 0])
    packed = jnp.concatenate(
        [qkv_bias[0, 0], zeros, qkv_bias[0, 1], fc1_bias[0], bias_table[0].T.reshape(-1)]
    )
    packed_other = swap(packed, "col")
    packed = jnp.where(
        col == 0, jnp.stack([packed, packed_other]), jnp.stack([packed_other, packed])
    )
    qb = packed[:, :768]
    b1 = packed[:, 768:1792].reshape(1, FF)
    table = packed[:, 1792:].reshape(HEADS, TABLE)
    pb, b2, gains, offs = proj_bias, fc2_bias, norm_gain[0], norm_bias[0]
    onehot = relative_onehot().astype(F32)
    rel = jnp.dot(table, onehot, precision=lax.Precision.HIGHEST).reshape(4, 4 * PAD, PAD)
    allow = allowed_cells(extents, section, col)
    place = jnp.where(
        first, jnp.asarray(place_matrix(count, 0), BF), jnp.asarray(place_matrix(count, SHIFT), BF)
    )

    def split(x):
        kept = x[:, 98 - KEPT :].reshape(KEEP, D)
        sent = x[:, : 98 - KEPT].reshape(-1, D)
        return jnp.concatenate([kept, jnp.pad(sent, ((0, SENT - sent.shape[0]), (0, 0)))], 0)

    def join(kept, sent):
        sent = sent[: count * (98 - KEPT)].reshape(count, 98 - KEPT, D)
        return jnp.concatenate([sent, kept.reshape(count, KEPT, D)], 1)

    line = lax.axis_size("dp") == 4
    dma = pltpu.SemaphoreType.DMA((12,))
    few = pltpu.SemaphoreType.DMA((5,))
    block = pltpu.VMEM((12, B, B), BF)
    tokens = pltpu.VMEM((rows, D), BF)
    wide = pltpu.VMEM((rows, D), F32)
    cells = pltpu.VMEM((KEEP + SENT, D), BF)
    part = pltpu.VMEM((SENT, D), BF)
    out_k, out_s, gin_k, gin_s, grads, small, tables = run(
        lambda *a: whole_step(win, line, *a),
        (
            split(images),
            split(cotangent),
            place,
            allow,
            rel,
            attn_w,
            mlp_w,
            qb,
            pb,
            b1.reshape(8, 1, B),
            b2,
            gains,
            offs,
        ),
        [
            ((KEEP, D), BF),
            ((SENT, D), BF),
            ((KEEP, D), BF),
            ((SENT, D), BF),
            ((12, B, B), BF),
            ((2, 8, D), F32),
            ((2, 4 * PAD, 2 * PAD), BF),
        ],
        "whole_step",
        6 * rows * D * (4 * D + 2 * FF),
        [
            pltpu.VMEM((2, 2, 4, B, B), BF),
            pltpu.VMEM((2, 2, 8, B, B), BF),
            tokens,
            pltpu.VMEM((2, rows, 768), BF),
            pltpu.VMEM((win * 4, 4 * PAD, PAD), F32),
            tokens,
            wide,
            tokens,
            tokens,
            pltpu.VMEM((8, rows, B), BF),
            pltpu.VMEM((8, rows, B), F32),
            pltpu.VMEM((8, rows, B), BF),
            tokens,
            wide,
            tokens,
            tokens,
            pltpu.VMEM((2, rows, 768), BF),
            cells,
            cells,
            cells,
            part,
            part,
            part,
            pltpu.VMEM((2, 2, 12, B, B), BF),
            pltpu.VMEM((12, 2, B, B), BF),
        ]
        + [block] * 6
        + [
            pltpu.VMEM((2, 8, D), F32),
            pltpu.VMEM((2, 4 * PAD, 2 * PAD), BF),
            pltpu.VMEM((7, 2, 8, D), F32),
            pltpu.VMEM((7, 2, 4 * PAD, 2 * PAD), BF),
        ]
        + [dma] * 6
        + [few] * 2
        + [dma] * 10
        + [pltpu.SemaphoreType.DMA((2, 5))] * 2,
        0,
    )
    layer_outputs = join(out_k, out_s)[None]
    input_grads = join(gin_k, gin_s)[None]
    if not line:
        grads, small, tables = lax.psum((grads, small, tables), "dp")
    grads = grads.astype(F32)
    g_mlp, g_attn = grads[:8], grads[8:]
    mine = lax.dynamic_index_in_dim(tables, col, 0, keepdims=False).astype(F32)
    mine = mine.reshape(4, PAD, 2, PAD).transpose(2, 0, 1, 3).reshape(HEADS // 2, PAD * PAD)
    table_grad = lax.dot_general(
        onehot, mine, (((1,), (1,)), ((), ())), precision=lax.Precision.HIGHEST
    )
    mlp_small, attn_small = small[0], small[1]
    b1_grad = lax.dynamic_slice_in_dim(mlp_small, 3 + 2 * col, 2, 0).reshape(1024)
    qkv_small = lax.dynamic_index_in_dim(
        attn_small[3:6].reshape(2, 3, B), col, 0, keepdims=False
    )
    qkv_bias_grad = jnp.stack([qkv_small[0], qkv_small[2]], 0)
    gain_grad = jnp.stack([attn_small[0], mlp_small[0]], 0)
    offset_grad = jnp.stack([attn_small[1], mlp_small[1]], 0)
    return (
        layer_outputs,
        input_grads,
        g_attn[:3].transpose(1, 0, 2)[None],
        qkv_bias_grad[None],
        g_attn[3][None],
        attn_small[2][None],
        g_mlp[:4].transpose(1, 0, 2).reshape(B, 1024)[None],
        b1_grad[None],
        g_mlp[4:].reshape(1024, B)[None],
        mlp_small[2][None],
        gain_grad[None],
        offset_grad[None],
        table_grad[None],
    )


def solution(mesh):
    placed = (
        P(("dp", "row"), "col", None),
        P(("dp", "row"), None),
        P(("dp", "row"), "col", None),
        P("pipe", "row", None, "col"),
        P("pipe", None, "col"),
        P("pipe", "col", "row"),
        P("pipe", None),
        P("pipe", "row", "col"),
        P("pipe", "col"),
        P("pipe", "col", "row"),
        P("pipe", None),
        P("pipe", None, None),
        P("pipe", None, None),
        P("pipe", None, "col"),
    )
    return jax.shard_map(
        per_device,
        mesh=mesh,
        in_specs=placed,
        out_specs=(
            P("pipe", ("dp", "row"), "col", None),
            P("pipe", ("dp", "row"), "col", None),
            P("pipe", "row", None, "col"),
            P("pipe", None, "col"),
            P("pipe", "col", "row"),
            P("pipe", None),
            P("pipe", "row", "col"),
            P("pipe", "col"),
            P("pipe", "col", "row"),
            P("pipe", None),
            P("pipe", None, None),
            P("pipe", None, None),
            P("pipe", None, "col"),
        ),
        check_vma=False,
    )
```

```python
import jax
import jax.numpy as jnp
import numpy as np
from jax import lax
from jax.experimental import pallas as pl
from jax.experimental.pallas import tpu as pltpu
from jax.sharding import PartitionSpec as P

D = 512
HEADS = 16
FF = 2048
HEAD_DIM = 32
WINDOW = 7
CELLS = 49
SIDE = 14
SHIFT = 3
SPAN = 13
TABLE = 169
PAD = 64
HALF_ROWS = 7
KEPT = 56
KEEP = 112
SENT = 96
B = 256
SCALE = HEAD_DIM ** (-0.5)
EPS = 1e-05
BLOCKED = -1000000000.0
BF = jnp.bfloat16
F32 = jnp.float32


def nn(a, b):
    return lax.dot_general(a, b, (((1,), (0,)), ((), ())), preferred_element_type=F32)


def nt(a, b):
    return lax.dot_general(a, b, (((1,), (1,)), ((), ())), preferred_element_type=F32)


def tn(a, b):
    return lax.dot_general(a, b, (((0,), (0,)), ((), ())), preferred_element_type=F32)


def norm_parts(values):
    mean = jnp.mean(values, -1, keepdims=True)
    centred = values - mean
    inv = lax.rsqrt(jnp.mean(centred * centred, -1, keepdims=True) + EPS)
    return centred * inv, inv


def norm_back(grad, values, gain):
    x, inv = norm_parts(values)
    s = grad * gain
    back = (s - jnp.mean(s, -1, keepdims=True) - x * jnp.mean(s * x, -1, keepdims=True)) * inv
    return back, x


def head_mask(dtype):
    lane = lax.broadcasted_iota(jnp.int32, (4 * PAD, 128), 1) // HEAD_DIM
    row = lax.broadcasted_iota(jnp.int32, (4 * PAD, 128), 0) // PAD
    return (lane == row).astype(F32).astype(dtype)


def four(x):
    return jnp.concatenate([x, x, x, x], axis=0)


def fold(x, mask):
    y = x * mask
    return y[:PAD] + y[PAD : 2 * PAD] + y[2 * PAD : 3 * PAD] + y[3 * PAD :]


def cut(j):
    return slice(j * B, (j + 1) * B)


def attn_fwd(win, h, allow, rel, w, qb, pb, gains, offs, normed, qkv, probs, mixed, middle):
    hv = h[...].astype(F32)
    x, _ = norm_parts(hv)
    nv = (x * gains[0:1] + offs[0:1]).astype(BF)
    normed[...] = nv
    for c in range(2):
        for t in range(3):
            acc = nn(nv[:, cut(0)], w[0, c, t]) + nn(nv[:, cut(1)], w[1, c, t])
            qkv[c, :, cut(t)] = (acc + qb[c : c + 1, cut(t)]).astype(BF)
    mask_low = head_mask(BF)
    mask = head_mask(F32)
    for c in range(2):
        for g in range(2):
            grp = 2 * c + g
            for n in range(win):
                rows = slice(n * PAD, (n + 1) * PAD)
                q = qkv[c, rows, g * 128 : g * 128 + 128]
                k = qkv[c, rows, B + g * 128 : B + g * 128 + 128]
                v = qkv[c, rows, 2 * B + g * 128 : 2 * B + g * 128 + 128]
                s = nt(four(q) * mask_low, k) * SCALE + rel[grp]
                s = jnp.where(allow[n] > 0.5, s, BLOCKED)
                e = jnp.exp(s - jnp.max(s, -1, keepdims=True))
                p = e / jnp.sum(e, -1, keepdims=True)
                probs[n * 4 + grp] = p
                o = fold(nn(p.astype(BF), v), mask)
                mixed[rows, grp * 128 : grp * 128 + 128] = o.astype(BF)
    mv = mixed[...]
    for r in range(2):
        acc = nn(mv[:, cut(0)], w[r, 0, 3]) + nn(mv[:, cut(1)], w[r, 1, 3])
        middle[:, cut(r)] = hv[:, cut(r)] + (acc + pb[:, cut(r)])


def partner_copy(src, dst, send, recv, device):
    return pltpu.make_async_remote_copy(
        src_ref=src,
        dst_ref=dst,
        send_sem=send,
        recv_sem=recv,
        device_id=device,
        device_id_type=pl.DeviceIdType.MESH,
    )


def greet(devices):
    barrier = pltpu.get_barrier_semaphore()
    for device in devices:
        pl.semaphore_signal(barrier, inc=1, device_id=device, device_id_type=pl.DeviceIdType.MESH)
    return barrier


def whole_step(win, line, *refs):
    (img, nat_cot, perm, place, allow, rel, la, lm, qb, pb, b1, b2, gains, offs) = refs[:14]
    (out_nat, gin_nat, grads, small_out, table_out) = refs[14:19]
    (wa, wm, normed, qkv, probs, mixed, middle, h, n2, act, dact, gpre, gz, gm, ga) = refs[19:34]
    (gmix, gqkv, grid, back, hop, cot, out_keep, cot_in, out_in, gin_in) = refs[34:44]
    (gbuf, rbuf, csend, cbuf, zsum, ebuf, wsum, mbuf) = refs[44:52]
    (small, table, hold_f, hold_b) = refs[52:56]
    (cs, cr, rs, rr, fs, fr, hs, hr) = refs[56:64]
    (rs2, rr2, cs2, cr2, es, er, ms, mr, bs, br, ps, pr) = refs[64:76]
    section = lax.axis_index("pipe")
    row, col, spot = lax.axis_index("row"), lax.axis_index("col"), lax.axis_index("dp")
    first, second = section == 0, section == 1
    to_row, to_col = {"row": 1 - row}, {"col": 1 - col}
    to_next, to_cross = {"pipe": 1 - section}, {"pipe": 1 - section, "col": 1 - col}
    inner = (spot == 1) | (spot == 2)
    outer = jnp.logical_not(inner)
    to_pair = {"dp": spot + 1 - 2 * lax.rem(spot, 2)}
    to_other = {"dp": 3 - spot}
    barrier = greet([to_row, to_col, to_next, to_cross, to_pair])
    if line:

        @pl.when(inner)
        def _():
            greet([to_other])
            pl.semaphore_wait(barrier, 6)

        @pl.when(outer)
        def _():
            pl.semaphore_wait(barrier, 5)
    else:
        pl.semaphore_wait(barrier, 5)

    odd = lax.rem(spot, 2)
    blocks = [(la, wa, k) for k in range(4)]
    for jj in range(2):
        blocks += [(lm, wm, 2 * jj + odd), (lm, wm, 4 + 2 * jj + odd)]
    over_col, onward, over_pair = [], [], []
    for i, (src, dst, k) in enumerate(blocks):
        over_col.append(
            partner_copy(src.at[k], dst.at[row, col, k], cs.at[i], cr.at[i], to_col)
        )
        far = dst.at[row, 1 - col, k]
        onward.append(partner_copy(far, far, fs.at[i], fr.at[i], to_row))
        if i >= 4:
            over_pair.append(partner_copy(far, far, cs.at[4 + i], cr.at[4 + i], to_pair))
        over_col[i].start()
    for jj in range(2):
        for q, k in enumerate((2 * jj + 1 - odd, 4 + 2 * jj + 1 - odd)):
            far = wm.at[row, 1 - col, k]
            i = 8 + 2 * jj + q
            onward.append(partner_copy(far, far, fs.at[i], fr.at[i], to_row))
    over_row = []
    for i in range(12):
        src, dst, k = (la, wa, i) if i < 4 else (lm, wm, i - 4)
        over_row.append(
            partner_copy(src.at[k], dst.at[row, col, k], rs.at[i], rr.at[i], to_row)
        )
        over_row[i].start()

    def arrive(jj):
        for i in (4 + 2 * jj, 5 + 2 * jj):
            over_col[i].wait_recv()
            onward[i].start()
            over_pair[i - 4].start()

    def arrive_pair(jj):
        for i in (2 * jj, 2 * jj + 1):
            over_pair[i].wait_recv()
            onward[8 + i].start()

    cot[...] = nn(perm[...], nat_cot[...]).astype(BF)
    cot_copy = partner_copy(cot.at[pl.ds(KEEP, SENT)], cot_in, hs.at[2], hr.at[2], to_col)
    cot_copy.start()
    wa[row, col] = la[...]
    wm[row, col] = lm[...]
    hop_keep = partner_copy(
        grid.at[pl.ds(0, KEEP)], hop.at[pl.ds(0, KEEP)], hs.at[0], hr.at[0], to_next
    )
    hop_cross = partner_copy(
        grid.at[pl.ds(KEEP, SENT)], hop.at[pl.ds(KEEP, SENT)], hs.at[1], hr.at[1], to_cross
    )
    for i in range(4):
        over_col[i].wait_recv()
        onward[i].start()
    for i in range(4):
        over_row[i].wait_recv()
        onward[i].wait_recv()

    @pl.when(first)
    def _():
        h[...] = nn(place[...], nn(perm[...], img[...]).astype(BF)).astype(BF)

    @pl.when(second)
    def _():
        for jj in range(2):
            arrive(jj)
        for jj in range(2):
            arrive_pair(jj)
        hop_keep.wait_recv()
        hop_cross.wait_recv()
        h[...] = nn(place[...], hop[...]).astype(BF)

    attn_fwd(win, h, allow, rel, wa, qb, pb, gains, offs, normed, qkv, probs, mixed, middle)
    mv = middle[...]
    x, _ = norm_parts(mv)
    nv = (x * gains[1:2] + offs[1:2]).astype(BF)
    n2[...] = nv
    acc = [mv[:, cut(r)] + b2[:, cut(r)] for r in range(2)]
    for near in range(2):
        c = col if near == 0 else 1 - col
        for step in range(4):
            if near == 0:
                j = step
                over_row[4 + j].wait_recv()
                over_row[8 + j].wait_recv()
                if step >= 2:

                    @pl.when(first)
                    def _():
                        arrive(step - 2)
            elif step < 2:
                j = 2 * step + odd
                onward[4 + 2 * step].wait_recv()
                onward[5 + 2 * step].wait_recv()
            else:
                jj = step - 2
                j = 2 * jj + 1 - odd

                @pl.when(first)
                def _():
                    arrive_pair(jj)

                onward[8 + 2 * jj].wait_recv()
                onward[9 + 2 * jj].wait_recv()
            at = c * 4 + j
            pre = nn(nv[:, cut(0)], wm[0, c, j]) + nn(nv[:, cut(1)], wm[1, c, j]) + b1[at]
            phi = 0.5 + 0.5 * lax.erf(pre * (0.5 ** 0.5))
            av = (pre * phi).astype(BF)
            act[at] = av
            dact[at] = phi + pre * (jnp.exp(-0.5 * pre * pre) * 0.3989422804014327)
            for r in range(2):
                acc[r] = acc[r] + nn(av, wm[r, c, 4 + j])
    outv = jnp.concatenate([acc[0].astype(BF), acc[1].astype(BF)], axis=1)
    grid[...] = tn(place[...], outv).astype(BF)
    out_copy = partner_copy(grid.at[pl.ds(KEEP, SENT)], out_in, hs.at[3], hr.at[3], to_col)

    @pl.when(first)
    def _():
        hop_keep.start()
        hop_cross.start()

    out_copy.start()
    out_keep[...] = grid[...]
    cot_copy.wait_recv()

    @pl.when(first)
    def _():
        hop_keep.wait_recv()
        hop_cross.wait_recv()
        gz[...] = nn(place[...], hop[...]).astype(BF)

    @pl.when(second)
    def _():
        back[:KEEP] = cot[:KEEP]
        back[KEEP:] = cot_in[...]
        gz[...] = nn(place[...], back[...]).astype(BF)

    zv = gz[...]
    gn = [None, None]
    small[...] = jnp.zeros_like(small)
    for c in range(2):
        for j in range(4):
            at = c * 4 + j
            gact = nt(zv[:, cut(0)], wm[0, c, 4 + j]) + nt(zv[:, cut(1)], wm[1, c, 4 + j])
            gp = (gact * dact[at]).astype(BF)
            gpre[at] = gp
            small[0, 3 + at // 2 : 4 + at // 2, cut(at % 2)] = jnp.sum(
                gp.astype(F32), 0, keepdims=True
            )
            for r in range(2):
                t = nt(gp, wm[r, c, j])
                gn[r] = t if gn[r] is None else gn[r] + t
    gnv = jnp.concatenate(gn, axis=1)
    inv_back, x = norm_back(gnv, middle[...], gains[1:2])
    gf = zv.astype(F32)
    gm[...] = gf + inv_back
    small[0, 0:1] = jnp.sum(gnv * x, 0, keepdims=True)
    small[0, 1:2] = jnp.sum(gnv, 0, keepdims=True)
    small[0, 2:3] = jnp.sum(gf, 0, keepdims=True)

    row_copies = [
        partner_copy(gbuf.at[1 - row, :, k], rbuf.at[k], rs2.at[k], rr2.at[k], to_row)
        for k in range(12)
    ]
    col_copies = [
        partner_copy(csend.at[k], cbuf.at[k], cs2.at[k], cr2.at[k], to_col) for k in range(12)
    ]

    def mlp_grads():
        for j in range(4):
            for r in range(2):
                for c in range(2):
                    gbuf[r, c, j] = tn(n2[:, cut(r)], gpre[c * 4 + j]).astype(BF)
                    gbuf[r, c, 4 + j] = tn(act[c * 4 + j], gz[:, cut(r)]).astype(BF)
            row_copies[j].start()
            row_copies[4 + j].start()

    def pass_on(ks):
        for k in ks:
            row_copies[k].wait_recv()
            other = gbuf[row, 1 - col, k].astype(F32) + rbuf[k, 1 - col].astype(F32)
            csend[k] = other.astype(BF)
            col_copies[k].start()

    order = (0, 4, 1, 5, 2, 6, 3, 7, 8, 9, 10, 11)

    @pl.when(first)
    def _():
        mlp_grads()

    ga[...] = gm[...].astype(BF)
    for c in range(2):
        part = nt(ga[:, cut(0)], wa[0, c, 3]) + nt(ga[:, cut(1)], wa[1, c, 3])
        gmix[:, cut(c)] = part.astype(BF)
    mask_low = head_mask(BF)
    mask = head_mask(F32)
    for c in range(2):
        tables = []
        for g in range(2):
            grp = 2 * c + g
            total = None
            for n in range(win):
                rows = slice(n * PAD, (n + 1) * PAD)
                q = qkv[c, rows, g * 128 : g * 128 + 128]
                k = qkv[c, rows, B + g * 128 : B + g * 128 + 128]
                v = qkv[c, rows, 2 * B + g * 128 : 2 * B + g * 128 + 128]
                g4 = four(gmix[rows, grp * 128 : grp * 128 + 128]) * mask_low
                p = probs[n * 4 + grp]
                gp = nt(g4, v)
                ds = (p * (gp - jnp.sum(p * gp, -1, keepdims=True))).astype(BF)
                gv = tn(p.astype(BF), g4)
                gq = fold(nn(ds, k), mask) * SCALE
                gk = tn(ds, four(q) * mask_low) * SCALE
                gqkv[c, rows, g * 128 : g * 128 + 128] = gq.astype(BF)
                gqkv[c, rows, B + g * 128 : B + g * 128 + 128] = gk.astype(BF)
                gqkv[c, rows, 2 * B + g * 128 : 2 * B + g * 128 + 128] = gv.astype(BF)
                total = ds.astype(F32) if total is None else total + ds.astype(F32)
            tables.append(total)
        table[c] = jnp.concatenate(tables, axis=1).astype(BF)
        if c == 0:

            @pl.when(first)
            def _():
                pass_on(order[:8])

    gn = [None, None]
    for c in range(2):
        for t in range(3):
            gt = gqkv[c, :, cut(t)]
            at = c * 3 + t
            small[1, 3 + at // 2 : 4 + at // 2, cut(at % 2)] = jnp.sum(
                gt.astype(F32), 0, keepdims=True
            )
            for r in range(2):
                part = nt(gt, wa[r, c, t])
                gn[r] = part if gn[r] is None else gn[r] + part
    gnv = jnp.concatenate(gn, axis=1)
    inv_back, x = norm_back(gnv, h[...].astype(F32), gains[0:1])
    gin = (gm[...] + inv_back).astype(BF)
    small[1, 0:1] = jnp.sum(gnv * x, 0, keepdims=True)
    small[1, 1:2] = jnp.sum(gnv, 0, keepdims=True)
    small[1, 2:3] = jnp.sum(ga[...].astype(F32), 0, keepdims=True)

    @pl.when(first)
    def _():
        hop_keep.wait_send()
        hop_cross.wait_send()

    out_copy.wait_send()
    grid[...] = tn(place[...], gin).astype(BF)

    @pl.when(second)
    def _():
        hop_keep.start()
        hop_cross.start()

    gin_copy = partner_copy(grid.at[pl.ds(KEEP, SENT)], gin_in, hs.at[4], hr.at[4], to_col)
    gin_copy.start()

    def shared_copies(own, hold, final, i):
        def copy(src, dst, step, device):
            return partner_copy(src, dst, ps.at[i, step], pr.at[i, step], device)

        return [
            copy(own, hold.at[0], 0, to_row),
            copy(hold.at[1], hold.at[2], 1, to_col),
            copy(hold.at[3], hold.at[4], 2, to_pair),
            copy(hold.at[5], hold.at[6], 3, to_other),
            copy(final, final, 4, to_pair),
        ][: 5 if line else 2]

    shared = [
        (small, hold_f, small_out, shared_copies(small, hold_f, small_out, 0)),
        (table, hold_b, table_out, shared_copies(table, hold_b, table_out, 1)),
    ]

    def plus(a, b, kind):
        return (a.astype(F32) + b.astype(F32)).astype(kind)

    for own, hold, final, copies in shared:
        copies[0].start()

    @pl.when(second)
    def _():
        mlp_grads()

    for r in range(2):
        for c in range(2):
            gbuf[r, c, 11] = tn(mixed[:, cut(c)], ga[:, cut(r)]).astype(BF)
    row_copies[11].start()
    for t in range(3):
        for r in range(2):
            for c in range(2):
                gbuf[r, c, 8 + t] = tn(normed[:, cut(r)], gqkv[c, :, cut(t)]).astype(BF)
        row_copies[8 + t].start()

    @pl.when(second)
    def _():
        pass_on(order[:8])

    for own, hold, final, copies in shared:
        copies[0].wait_recv()
        hold[1] = plus(own[...], hold[0], hold.dtype)
        copies[1].start()
    pass_on(order[8:])

    to_inner = [partner_copy(zsum.at[k], ebuf.at[k], es.at[k], er.at[k], to_pair) for k in order]
    across = [partner_copy(wsum.at[k], mbuf.at[k], ms.at[k], mr.at[k], to_other) for k in order]
    to_outer = [partner_copy(grads.at[k], grads.at[k], bs.at[k], br.at[k], to_pair) for k in order]
    for t in range(15 if line else 13):
        if t < 12:
            k = order[t]
            col_copies[k].wait_recv()
            mine = gbuf[row, col, k].astype(F32) + rbuf[k, col].astype(F32)
            total = (mine + cbuf[k].astype(F32)).astype(BF)
            if line:
                zsum[k] = total

                @pl.when(outer)
                def _():
                    to_inner[t].start()
            else:
                grads[k] = total
        if t == 12:
            for own, hold, final, copies in shared:
                copies[1].wait_recv()
                total = plus(hold[1], hold[2], hold.dtype)
                if line:
                    hold[3] = total

                    @pl.when(outer)
                    def _():
                        copies[2].start()
                else:
                    final[...] = total
        if not line:
            continue

        @pl.when(inner)
        def _():
            if 1 <= t < 13:
                k = order[t - 1]
                to_inner[t - 1].wait_recv()
                wsum[k] = plus(zsum[k], ebuf[k], BF)
                across[t - 1].start()
            if t == 13:
                for own, hold, final, copies in shared:
                    copies[2].wait_recv()
                    hold[5] = plus(hold[3], hold[4], hold.dtype)
                    copies[3].start()
            if 2 <= t < 14:
                k = order[t - 2]
                across[t - 2].wait_recv()
                grads[k] = plus(wsum[k], mbuf[k], BF)
                to_outer[t - 2].start()
            if t == 14:
                for own, hold, final, copies in shared:
                    copies[3].wait_recv()
                    final[...] = plus(hold[5], hold[6], hold.dtype)
                    copies[4].start()

    out_copy.wait_recv()
    gin_copy.wait_recv()

    @pl.when(second)
    def _():
        hop_keep.wait_send()
        hop_cross.wait_send()

    gin_copy.wait_send()

    @pl.when(second)
    def _():
        out_keep[KEEP:] = out_in[...]
        grid[KEEP:] = gin_in[...]

    out_nat[...] = tn(perm[...], out_keep[...]).astype(BF)
    gin_nat[...] = tn(perm[...], grid[...]).astype(BF)
    cot_copy.wait_send()
    for i in range(8):
        over_col[i].wait_send()
    for i in range(4):
        over_pair[i].wait_send()
    for i in range(12):
        over_row[i].wait_send()
        onward[i].wait_send()
        row_copies[i].wait_send()
        col_copies[i].wait_send()
    for own, hold, final, copies in shared:
        copies[0].wait_send()
        copies[1].wait_send()
    if line:

        @pl.when(outer)
        def _():
            for i in range(12):
                to_outer[i].wait_recv()
                to_inner[i].wait_send()
            for own, hold, final, copies in shared:
                copies[4].wait_recv()
                copies[2].wait_send()

        @pl.when(inner)
        def _():
            for i in range(12):
                across[i].wait_send()
                to_outer[i].wait_send()
            for own, hold, final, copies in shared:
                copies[3].wait_send()
                copies[4].wait_send()


def run(body, args, outs, name, flops, scratch=(), shared=None):
    shapes = [jax.ShapeDtypeStruct(s, d) for s, d in outs]
    moved = sum(a.size * a.dtype.itemsize for a in list(args) + shapes)
    vm = pl.BlockSpec(memory_space=pltpu.VMEM)
    return pl.pallas_call(
        body,
        out_shape=shapes,
        in_specs=[vm] * len(args),
        out_specs=[vm] * len(outs),
        scratch_shapes=list(scratch),
        compiler_params=pltpu.CompilerParams(
            vmem_limit_bytes=56 * 1024 * 1024,
            collective_id=shared,
            has_side_effects=shared is not None,
        ),
        cost_estimate=pl.CostEstimate(flops=flops, bytes_accessed=moved, transcendentals=0),
        name=name,
    )(*args)


def place_matrix(images, shift):
    out = np.zeros((images * 2 * PAD, KEEP + SENT), np.float32)
    for n in range(images):
        for r in range(HALF_ROWS):
            kept = r < 4 if shift else r >= SHIFT
            for c in range(SIDE):
                rolled = (c - shift) % SIDE
                row = (n * 2 + rolled // WINDOW) * PAD + r * WINDOW + rolled % WINDOW
                if kept:
                    at = n * 56 + (r if shift else r - SHIFT) * SIDE + c
                else:
                    at = KEEP + n * 42 + (r - 4 if shift else r) * SIDE + c
                out[row, at] = 1.0
    return out


def allowed_cells(extents, section, col):
    images = extents.shape[0]
    places = jnp.arange(SIDE, dtype=jnp.int32)
    source = (places + SHIFT * section) % SIDE
    padded = (source[None, :, None] >= extents[:, 0, None, None]) | (
        source[None, None, :] >= extents[:, 1, None, None]
    )
    band = (places >= SIDE - WINDOW).astype(jnp.int32) + (places >= SIDE - SHIFT).astype(jnp.int32)
    codes = (band[:, None] * 3 + band[None, :]) * section * 2 + padded.astype(jnp.int32)
    mine = lax.dynamic_slice_in_dim(codes, col * HALF_ROWS, HALF_ROWS, 1)
    mine = mine.reshape(images, HALF_ROWS, 2, WINDOW).transpose(0, 2, 1, 3)
    mine = mine.reshape(images * 2, CELLS)
    query = jnp.pad(mine, ((0, 0), (0, PAD - CELLS)))
    key = jnp.pad(mine, ((0, 0), (0, PAD - CELLS)), constant_values=-1)
    real = jnp.arange(PAD) < CELLS
    same = (query[:, :, None] == key[:, None, :]) | ((~real)[None, :, None] & real[None, None, :])
    return jnp.tile(same.astype(F32), (1, 4, 1))


def relative_onehot():
    cells = np.arange(CELLS)
    a, b = cells // WINDOW, cells % WINDOW
    index = (a[:, None] - a[None, :] + WINDOW - 1) * SPAN + b[:, None] - b[None, :] + WINDOW - 1
    full = np.full((PAD, PAD), -1, np.int32)
    full[:CELLS, :CELLS] = index
    return jnp.asarray(full.reshape(-1))[None, :] == jnp.arange(TABLE, dtype=jnp.int32)[:, None]


def per_device(
    images,
    extents,
    cotangent,
    qkv_weight,
    qkv_bias,
    proj_weight,
    proj_bias,
    fc1_weight,
    fc1_bias,
    fc2_weight,
    fc2_bias,
    norm_gain,
    norm_bias,
    bias_table,
):
    section = lax.axis_index("pipe")
    row = lax.axis_index("row")
    col = lax.axis_index("col")
    first = section == 0
    count = images.shape[0]
    win = count * 2
    rows = win * PAD

    def swap(x, axis):
        return lax.ppermute(x, axis, [(0, 1), (1, 0)])

    attn_w = jnp.concatenate(
        [qkv_weight[0].transpose(1, 0, 2), proj_weight], axis=0
    )
    mlp_w = jnp.concatenate(
        [fc1_weight[0].reshape(B, 4, B).transpose(1, 0, 2), fc2_weight[0].reshape(4, B, B)], axis=0
    )

    zeros = jnp.zeros_like(qkv_bias[0, 0])
    packed = jnp.concatenate(
        [qkv_bias[0, 0], zeros, qkv_bias[0, 1], fc1_bias[0], bias_table[0].T.reshape(-1)]
    )
    packed_other = swap(packed, "col")
    packed = jnp.where(
        col == 0, jnp.stack([packed, packed_other]), jnp.stack([packed_other, packed])
    )
    qb = packed[:, :768]
    b1 = packed[:, 768:1792].reshape(1, FF)
    table = packed[:, 1792:].reshape(HEADS, TABLE)
    pb, b2, gains, offs = proj_bias, fc2_bias, norm_gain[0], norm_bias[0]
    onehot = relative_onehot().astype(F32)
    rel = jnp.dot(table, onehot, precision=lax.Precision.HIGHEST).reshape(4, 4 * PAD, PAD)
    allow = allowed_cells(extents, section, col)
    place = jnp.where(
        first, jnp.asarray(place_matrix(count, 0), BF), jnp.asarray(place_matrix(count, SHIFT), BF)
    )

    order = np.zeros((KEEP + SENT, count * 98), np.float32)
    for n in range(count):
        for r in range(98):
            at = KEEP + n * 42 + r if r < 42 else n * 56 + r - 42
            order[at, n * 98 + r] = 1.0
    perm = jnp.asarray(order, BF)
    line = lax.axis_size("dp") == 4
    dma = pltpu.SemaphoreType.DMA((12,))
    few = pltpu.SemaphoreType.DMA((5,))
    block = pltpu.VMEM((12, B, B), BF)
    tokens = pltpu.VMEM((rows, D), BF)
    wide = pltpu.VMEM((rows, D), F32)
    cells = pltpu.VMEM((KEEP + SENT, D), BF)
    part = pltpu.VMEM((SENT, D), BF)
    out_nat, gin_nat, grads, small, tables = run(
        lambda *a: whole_step(win, line, *a),
        (
            images.reshape(count * 98, D),
            cotangent.reshape(count * 98, D),
            perm,
            place,
            allow,
            rel,
            attn_w,
            mlp_w,
            qb,
            pb,
            b1.reshape(8, 1, B),
            b2,
            gains,
            offs,
        ),
        [
            ((count * 98, D), BF),
            ((count * 98, D), BF),
            ((12, B, B), BF),
            ((2, 8, D), F32),
            ((2, 4 * PAD, 2 * PAD), BF),
        ],
        "whole_step",
        6 * rows * D * (4 * D + 2 * FF),
        [
            pltpu.VMEM((2, 2, 4, B, B), BF),
            pltpu.VMEM((2, 2, 8, B, B), BF),
            tokens,
            pltpu.VMEM((2, rows, 768), BF),
            pltpu.VMEM((win * 4, 4 * PAD, PAD), F32),
            tokens,
            wide,
            tokens,
            tokens,
            pltpu.VMEM((8, rows, B), BF),
            pltpu.VMEM((8, rows, B), F32),
            pltpu.VMEM((8, rows, B), BF),
            tokens,
            wide,
            tokens,
            tokens,
            pltpu.VMEM((2, rows, 768), BF),
            cells,
            cells,
            cells,
            cells,
            cells,
            part,
            part,
            part,
            pltpu.VMEM((2, 2, 12, B, B), BF),
            pltpu.VMEM((12, 2, B, B), BF),
        ]
        + [block] * 6
        + [
            pltpu.VMEM((2, 8, D), F32),
            pltpu.VMEM((2, 4 * PAD, 2 * PAD), BF),
            pltpu.VMEM((7, 2, 8, D), F32),
            pltpu.VMEM((7, 2, 4 * PAD, 2 * PAD), BF),
        ]
        + [dma] * 6
        + [few] * 2
        + [dma] * 10
        + [pltpu.SemaphoreType.DMA((2, 5))] * 2,
        0,
    )
    layer_outputs = out_nat.reshape(images.shape)[None]
    input_grads = gin_nat.reshape(images.shape)[None]
    if not line:
        grads, small, tables = lax.psum((grads, small, tables), "dp")
    grads = grads.astype(F32)
    g_mlp, g_attn = grads[:8], grads[8:]
    mine = lax.dynamic_index_in_dim(tables, col, 0, keepdims=False).astype(F32)
    mine = mine.reshape(4, PAD, 2, PAD).transpose(2, 0, 1, 3).reshape(HEADS // 2, PAD * PAD)
    table_grad = lax.dot_general(
        onehot, mine, (((1,), (1,)), ((), ())), precision=lax.Precision.HIGHEST
    )
    mlp_small, attn_small = small[0], small[1]
    b1_grad = lax.dynamic_slice_in_dim(mlp_small, 3 + 2 * col, 2, 0).reshape(1024)
    qkv_small = lax.dynamic_index_in_dim(
        attn_small[3:6].reshape(2, 3, B), col, 0, keepdims=False
    )
    qkv_bias_grad = jnp.stack([qkv_small[0], qkv_small[2]], 0)
    gain_grad = jnp.stack([attn_small[0], mlp_small[0]], 0)
    offset_grad = jnp.stack([attn_small[1], mlp_small[1]], 0)
    return (
        layer_outputs,
        input_grads,
        g_attn[:3].transpose(1, 0, 2)[None],
        qkv_bias_grad[None],
        g_attn[3][None],
        attn_small[2][None],
        g_mlp[:4].transpose(1, 0, 2).reshape(B, 1024)[None],
        b1_grad[None],
        g_mlp[4:].reshape(1024, B)[None],
        mlp_small[2][None],
        gain_grad[None],
        offset_grad[None],
        table_grad[None],
    )


def solution(mesh):
    placed = (
        P(("dp", "row"), "col", None),
        P(("dp", "row"), None),
        P(("dp", "row"), "col", None),
        P("pipe", "row", None, "col"),
        P("pipe", None, "col"),
        P("pipe", "col", "row"),
        P("pipe", None),
        P("pipe", "row", "col"),
        P("pipe", "col"),
        P("pipe", "col", "row"),
        P("pipe", None),
        P("pipe", None, None),
        P("pipe", None, None),
        P("pipe", None, "col"),
    )
    return jax.shard_map(
        per_device,
        mesh=mesh,
        in_specs=placed,
        out_specs=(
            P("pipe", ("dp", "row"), "col", None),
            P("pipe", ("dp", "row"), "col", None),
            P("pipe", "row", None, "col"),
            P("pipe", None, "col"),
            P("pipe", "col", "row"),
            P("pipe", None),
            P("pipe", "row", "col"),
            P("pipe", "col"),
            P("pipe", "col", "row"),
            P("pipe", None),
            P("pipe", None, None),
            P("pipe", None, None),
            P("pipe", None, "col"),
        ),
        check_vma=False,
    )
```
